128 devices in a mesh: dp: 8 (over x, core), mp: 16 (over z, y).
Axes of the slice: x: 4, y: 4, z: 4, core: 2. Of those that a mesh axis runs over, the one named last changes fastest.
Arguments:
- gradient: float32 [256, 512, 512], P('mp', 'dp')
- owner: int32 [256], replicated, may hold values from 0 to 127, as said below
- stat_left: float32 [8, 16, 3, 512, 512], P('dp', 'mp'), as said below
- stat_right: float32 [8, 16, 3, 512, 512], P('dp', 'mp'), as said below
- root_left: bfloat16 [8, 16, 3, 512, 512], P('dp', 'mp'), as said below
- root_right: bfloat16 [8, 16, 3, 512, 512], P('dp', 'mp'), as said below
Outputs:
- preconditioned: float32 [256, 512, 512], P('mp', 'dp')
- new_stat_left: float32 [8, 16, 3, 512, 512], P('dp', 'mp')
- new_stat_right: float32 [8, 16, 3, 512, 512], P('dp', 'mp')
- new_root_left: bfloat16 [8, 16, 3, 512, 512], P('dp', 'mp')
- new_root_right: bfloat16 [8, 16, 3, 512, 512], P('dp', 'mp')
The draws below stay inside these ranges and needn't reach their ends.
Inputs may be any that keep to these rules, and one draw needn't show every extreme that they name: Each entry is a device e * 16 + h. Of the blocks of set g, exactly one has its owner's mp index equal to h, for every g and h. Every device owns at most 3 blocks and some device of every mp index owns exactly 3. `stat_left`: each matrix is symmetric with a positive diagonal that exceeds the sum of the magnitudes of its row's other entries. `stat_right`: each matrix is symmetric with a positive diagonal that exceeds the sum of the magnitudes of its row's other entries. `root_left`: each matrix is symmetric. `root_right`: each matrix is symmetric.
All inputs are finite; a program needn't handle non-finite values.
Results may differ from the reference program's by a relative error of at most 0.001.
Values sent between devices are 32-bit elements; how exact they have to be, the bound alone decides.
A program may use at most 192 MiB of HBM per device.

```python
import math
import jax
import jax.numpy as jnp
from jax import lax

BLOCK = 512
OWN = 3
RANKS = 8
GROUPS = 16
BLOCKS = 256


def draw_gradient(key, part):
    key = jax.random.fold_in(key, 2)
    first_key, second_key = jax.random.split(key, 2)
    shape = (BLOCKS, BLOCK, BLOCK)
    column_scale = jnp.exp(jax.random.uniform(second_key, (BLOCKS, 1, BLOCK), jnp.float32, math.log(0.3), math.log(3.0)))
    values = jax.random.normal(first_key, shape, jnp.float32)
    return values * column_scale


def mirrored(values):
    order_size = values.shape[-1]
    upper = jnp.arange(order_size)[:, None] < jnp.arange(order_size)[None, :]
    return jnp.where(upper, values, jnp.swapaxes(values, -1, -2))


def statistic_draw(key, lower, upper, spread):
    second_key = jax.random.fold_in(key, 1)
    shape = (RANKS, GROUPS, OWN, BLOCK, BLOCK)
    off_part = mirrored(spread)
    diag_values = jax.random.uniform(second_key, shape[:-1], jnp.float32, lower * BLOCK, upper * BLOCK)
    identity = jnp.eye(BLOCK, dtype=jnp.float32)
    return off_part * (1.0 - identity) + identity * diag_values[..., None]


def draw_stat_left(key, part):
    key = jax.random.fold_in(key, 3)
    first_key, second_key = jax.random.split(key)
    shape = (RANKS, GROUPS, OWN, BLOCK, BLOCK)
    spread = jax.random.truncated_normal(first_key, -2.5, 2.5, shape, jnp.float32)
    return statistic_draw(second_key, 2.6, 4.0, spread)


def draw_stat_right(key, part):
    key = jax.random.fold_in(key, 4)
    first_key, second_key = jax.random.split(key)
    shape = (RANKS, GROUPS, OWN, BLOCK, BLOCK)
    spread = jax.random.truncated_normal(first_key, -2.5, 2.5, shape, jnp.float32)
    return statistic_draw(second_key, 2.6, 4.0, spread)


def root_draw(key, spread):
    shape = (RANKS, GROUPS, OWN, BLOCK, BLOCK)
    off_part = mirrored(spread) * (0.11 / math.sqrt(BLOCK))
    diag_values = jax.random.uniform(key, shape[:-1], jnp.float32, 0.8, 1.2)
    identity = jnp.eye(BLOCK, dtype=jnp.float32)
    return (off_part * (1.0 - identity) + identity * diag_values[..., None]).astype(jnp.bfloat16)


def draw_root_left(key, part):
    key = jax.random.fold_in(key, 5)
    first_key, second_key = jax.random.split(key)
    shape = (RANKS, GROUPS, OWN, BLOCK, BLOCK)
    spread = jax.random.truncated_normal(first_key, -3.0, 3.0, shape, jnp.float32)
    return root_draw(second_key, spread)


def draw_root_right(key, part):
    key = jax.random.fold_in(key, 6)
    first_key, second_key = jax.random.split(key)
    shape = (RANKS, GROUPS, OWN, BLOCK, BLOCK)
    spread = jax.random.truncated_normal(first_key, -3.0, 3.0, shape, jnp.float32)
    return root_draw(second_key, spread)


def draw_owner(key, part):
    key = jax.random.fold_in(key, 7)
    first_key, second_key, third_key = jax.random.split(key, 3)
    dest_group = jax.vmap(lambda sub_key: jax.random.permutation(sub_key, GROUPS))(jax.random.split(first_key, GROUPS))
    pattern = jnp.tile(jnp.array([3, 2, 2, 1], jnp.int32), RANKS // 4)
    loads = jax.vmap(lambda sub_key: jax.random.permutation(sub_key, pattern))(jax.random.split(second_key, GROUPS))
    bounds = jnp.cumsum(loads, axis=1)
    position = jax.vmap(lambda sub_key: jax.random.permutation(sub_key, GROUPS))(jax.random.split(third_key, GROUPS))
    source_index = jnp.broadcast_to(jnp.arange(GROUPS, dtype=jnp.int32)[:, None], (GROUPS, GROUPS))
    place = position[dest_group, source_index]
    rank_index = jnp.sum((place[..., None] >= bounds[dest_group]).astype(jnp.int32), axis=-1)
    return (rank_index * GROUPS + dest_group).reshape(BLOCKS).astype(jnp.int32)


def setup_inputs(seed: int = 0) -> dict:
    seeds = jax.random.split(jax.random.key(seed), 7)
    gradient = draw_gradient(jax.random.fold_in(seeds[6], 71), 0)
    owner = draw_owner(jax.random.fold_in(seeds[6], 71), 0)
    stat_left = draw_stat_left(jax.random.fold_in(seeds[6], 71), 0)
    stat_right = draw_stat_right(jax.random.fold_in(seeds[6], 71), 0)
    root_left = draw_root_left(jax.random.fold_in(seeds[6], 71), 0)
    root_right = draw_root_right(jax.random.fold_in(seeds[6], 71), 0)
    return dict(gradient=gradient, owner=owner, stat_left=stat_left, stat_right=stat_right, root_left=root_left, root_right=root_right)


decay_rate = 0.95
damping = 0.001


def matmul_high(left_matrix, right_matrix):
    return jnp.matmul(left_matrix, right_matrix, precision=lax.Precision.HIGHEST)


def newton_step(statistic, old_root):
    size_order = statistic.shape[0]
    identity = jnp.eye(size_order, dtype=jnp.float32)
    scale = jnp.trace(statistic) / size_order
    shifted = statistic / scale + damping * identity
    square = matmul_high(old_root, old_root)
    power = matmul_high(matmul_high(square, square), shifted)
    return matmul_high(old_root, (5.0 * identity - power) / 4.0)


def refresh_block(grad_block, old_left, old_right, prev_left, prev_right):
    left_new = decay_rate * old_left + matmul_high(grad_block, grad_block.T)
    right_new = decay_rate * old_right + matmul_high(grad_block.T, grad_block)
    inverse_left = newton_step(left_new, prev_left.astype(jnp.float32))
    inverse_right = newton_step(right_new, prev_right.astype(jnp.float32))
    result = matmul_high(matmul_high(inverse_left, grad_block), inverse_right)
    return result, left_new, right_new, inverse_left.astype(jnp.bfloat16), inverse_right.astype(jnp.bfloat16)


def reference(gradient, owner, stat_left, stat_right, root_left, root_right):
    total_slots = RANKS * GROUPS * OWN
    earlier = jnp.arange(BLOCKS)[:, None] > jnp.arange(BLOCKS)[None, :]
    same_owner = owner[:, None] == owner[None, :]
    slot_rank = jnp.sum(jnp.logical_and(earlier, same_owner), axis=1).astype(jnp.int32)
    flat_index = (owner * OWN + slot_rank).astype(jnp.int32)
    flat_shape = (total_slots, BLOCK, BLOCK)
    left_flat = stat_left.reshape(flat_shape)
    right_flat = stat_right.reshape(flat_shape)
    rootl_flat = root_left.reshape(flat_shape)
    rootr_flat = root_right.reshape(flat_shape)

    def per_block(item):
        grad_block, position = item
        return refresh_block(grad_block, left_flat[position], right_flat[position], rootl_flat[position], rootr_flat[position])

    result, left_new, right_new, inv_left, inv_right = lax.map(per_block, (gradient, flat_index))
    full_shape = stat_left.shape
    new_left = jnp.zeros(flat_shape, jnp.float32).at[flat_index].set(left_new).reshape(full_shape)
    new_right = jnp.zeros(flat_shape, jnp.float32).at[flat_index].set(right_new).reshape(full_shape)
    out_left = jnp.zeros(flat_shape, jnp.bfloat16).at[flat_index].set(inv_left).reshape(full_shape)
    out_right = jnp.zeros(flat_shape, jnp.bfloat16).at[flat_index].set(inv_right).reshape(full_shape)
    return result, new_left, new_right, out_left, out_right
```

```python
import functools

import jax
import jax.numpy as jnp
from jax import lax
from jax.experimental import pallas as pl
from jax.experimental.pallas import tpu as pltpu
from jax.sharding import PartitionSpec as P

MESH = pl.DeviceIdType.MESH
N = 512
ROWS = 64
OWN = 3
RANKS = 8
GROUPS = 16
SIDE = 4
GATHER = ((0, 16), (16, 16), (32, 16), (48, 16))
RETURN = ((0, 16), (16, 16), (32, 16), (48, 16))
LATE = 2
TINY = 2.0**-48

SEND1, SLOT2, SLOT3, ORDER4, LIVE = 0, 16, 40, 56, 72


def tables(owner, group, rank):
    table = owner.reshape(GROUPS, GROUPS)
    of_group, of_rank = table % GROUPS, table // GROUPS
    each = jnp.arange(GROUPS, dtype=jnp.int32)

    def away(target, source):
        dz = (target // SIDE - source // SIDE) % SIDE
        dy = (target % SIDE - source % SIDE) % SIDE
        return dz * SIDE + dy

    mine = lax.dynamic_index_in_dim(of_group, group, 0, keepdims=False)
    sent_to = away(mine, group)
    send1 = jnp.sum(jnp.where(sent_to[None, :] == each[:, None], each[None, :], 0), axis=1)
    rank_of = jnp.sum(jnp.where(of_group == group, of_rank, 0), axis=1)
    before = (rank_of[:, None] == rank_of[None, :]) & (each[:, None] > each[None, :])
    slot_of = jnp.sum(before.astype(jnp.int32), axis=1)
    place = rank_of * OWN + slot_of
    came = away(group, each)
    places = jnp.arange(RANKS * OWN, dtype=jnp.int32)
    hit = place[None, :] == places[:, None]
    slot2 = jnp.sum(jnp.where(hit, came[None, :], 0), axis=1)
    goes = away(each, group)
    back = slot_of * RANKS + rank_of
    slot3 = jnp.sum(jnp.where(goes[None, :] == each[:, None], back[None, :], 0), axis=1)
    order4 = away(group, mine)
    slots = jnp.arange(OWN, dtype=jnp.int32)
    live = jnp.any(place[None, :] == (rank * OWN + slots)[:, None], axis=1).astype(jnp.int32)
    return jnp.concatenate([send1, slot2, slot3, order4, live]).astype(jnp.int32)


def split(x):
    high = x.astype(jnp.bfloat16)
    return high, (x - high.astype(jnp.float32)).astype(jnp.bfloat16)


def dot(a, b):
    return jnp.dot(a, b, preferred_element_type=jnp.float32)


def dot3(a, b):
    (ah, al), (bh, bl) = a, b
    return dot(ah, bh) + (dot(ah, bl) + dot(al, bh))


def kernel(tab, grad, stat_l, stat_r, root_l, root_r, out, new_sl, new_sr, new_rl, new_rr, *scratch):
    ng, nr = len(GATHER), len(RETURN)
    scratch = list(scratch)
    take = lambda count: [scratch.pop(0) for _ in range(count)]
    staged, recv1, recv3, recv4 = take(ng), take(ng), take(nr), take(nr)
    send1, send2, gbuf, send3, send4, outv, st, rt, x5 = take(9)
    in_sem, out_sem, s1, r1, s2, r2, s3, r3, s4, r4 = take(10)

    rank, group = lax.axis_index("dp"), lax.axis_index("mp")
    z, y = group // SIDE, group % SIDE

    def mp_peer(k):
        return (rank, ((z + k // SIDE) % SIDE) * SIDE + (y + k % SIDE) % SIDE)

    def dp_peer(d):
        return ((rank + d) % RANKS, group)

    def remote(src, dst, ssem, rsem, peer):
        return pltpu.make_async_remote_copy(
            src_ref=src, dst_ref=dst, send_sem=ssem, recv_sem=rsem, device_id=peer, device_id_type=MESH
        )

    def wait_recv(region, sem):
        remote(region, region, s1, sem, dp_peer(1)).wait_recv()

    def wait_send(region, sem):
        remote(region, region, sem, r1.at[0], dp_peer(1)).wait_send()

    grad_in = [
        pltpu.make_async_copy(grad.at[:, pl.ds(a, n), :], staged[i], in_sem.at[i]) for i, (a, n) in enumerate(GATHER)
    ]
    state_in = [
        pltpu.make_async_copy(src.at[0, 0], dst, in_sem.at[ng + i])
        for i, (src, dst) in enumerate(
            ((root_l, rt.at[0]), (root_r, rt.at[1]), (stat_l, st.at[0]), (stat_r, st.at[1]))
        )
    ]
    for copy in grad_in + state_in:
        copy.start()

    barrier = pltpu.get_barrier_semaphore()

    def greet_mp(k, carry):
        pl.semaphore_signal(barrier, inc=1, device_id=mp_peer(k), device_id_type=MESH)
        return carry

    def greet_dp(d, carry):
        pl.semaphore_signal(barrier, inc=1, device_id=dp_peer(d), device_id_type=MESH)
        return carry

    lax.fori_loop(1, GROUPS, greet_mp, 0)
    lax.fori_loop(1, RANKS, greet_dp, 0)
    pl.semaphore_wait(barrier, GROUPS - 1 + RANKS - 1)

    for i, (a, n) in enumerate(GATHER):
        grad_in[i].wait()
        rows = pl.ds(a, n)
        recv1[i][0] = staged[i][tab[SEND1]]

        def step1(k, carry, i=i, rows=rows):
            send1[k, rows, :] = staged[i][tab[SEND1 + k]]
            remote(send1.at[k, rows], recv1[i].at[k], s1, r1.at[i], mp_peer(k)).start()
            return carry

        lax.fori_loop(1, GROUPS, step1, 0)

    def second(i, slots, fill):
        a, n = GATHER[i]
        rows = pl.ds(a, n)

        def step2(d, carry):
            peer = (rank + d) % RANKS
            for s in slots:
                if fill:
                    send2[d * OWN + s, rows, :] = recv1[i][tab[SLOT2 + peer * OWN + s]]
                remote(send2.at[d * OWN + s, rows], gbuf.at[s, rank, rows], s2, r2.at[s], dp_peer(d)).start()
            return carry

        lax.fori_loop(1, RANKS, step2, 0)

    def own_rows(i):
        a, n = GATHER[i]
        for s in range(OWN):
            gbuf[s, rank, pl.ds(a, n), :] = recv1[i][tab[SLOT2 + rank * OWN + s]]

    def power(t, carry):
        side, s = t // OWN, t % OWN
        x = rt[side, s]
        sq = split(dot(x, x))
        fourth = split(dot3(sq, sq) * TINY)
        high, low = split(dot(x, fourth[0]) + dot(x, fourth[1]))
        x5[side, s, 0] = high
        x5[side, s, 1] = low
        return carry

    units = 2 * OWN
    for i, (a, n) in enumerate(GATHER):
        wait_recv(recv1[i].at[pl.ds(1, GROUPS - 1)], r1.at[i])
        second(i, (0, 1, 2) if i < LATE else (0, 1), True)
        if i == ng - 1:
            for late in range(LATE, ng):
                second(late, (2,), True)
        own_rows(i)
        if i == 0:
            state_in[0].wait()
            state_in[1].wait()
        first, last = units * i // (ng - 1), units * (i + 1) // (ng - 1)
        if i < ng - 1:
            lax.fori_loop(first, last, power, 0)
    state_in[2].wait()
    state_in[3].wait()

    eye = lax.broadcasted_iota(jnp.int32, (N, N), 0) == lax.broadcasted_iota(jnp.int32, (N, N), 1)

    def newton(side, s, new, taken):
        scale = jnp.sum(jnp.where(eye, new, 0.0)) / N
        shifted = split(new / scale + jnp.where(eye, 0.001, 0.0))
        moved = dot3((x5[side, s, 0], x5[side, s, 1]), shifted)
        inverse = 1.25 * rt[side, s].astype(jnp.float32) - (0.25 / TINY) * moved
        st[side, s] = jnp.where(taken, new, 0.0)
        rt[side, s] = jnp.where(taken, inverse, 0.0).astype(jnp.bfloat16)
        return inverse

    def refresh(s, carry):
        wait_recv(gbuf.at[s, pl.ds(0, RANKS - 1)], r2.at[s])
        taken = tab[LIVE + s] > 0
        g32 = gbuf[s].reshape(N, N)
        g, gt = split(g32), split(g32.T)
        inv_l = newton(0, s, 0.95 * st[0, s] + dot3(g, gt), taken)
        inv_r = newton(1, s, 0.95 * st[1, s] + dot3(gt, g), taken)
        result = dot3(split(dot3(split(inv_l), g)), split(inv_r))
        send3[pl.ds(s * RANKS, RANKS)] = result.reshape(RANKS, ROWS, N)
        for i, (a, n) in enumerate(RETURN):
            rows = pl.ds(a, n)

            def step3(d, carry, i=i, rows=rows):
                peer = (rank + d) % RANKS
                remote(
                    send3.at[s * RANKS + peer, rows], recv3[i].at[s * RANKS + rank], s3, r3.at[i], dp_peer(d)
                ).start()
                return carry

            lax.fori_loop(1, RANKS, step3, 0)
            recv3[i][s * RANKS + rank] = send3[s * RANKS + rank, rows, :]
        for side, (stat, root) in enumerate(((new_sl, new_rl), (new_sr, new_rr))):
            pltpu.make_async_copy(st.at[side, s], stat.at[0, 0, s], out_sem.at[0, side, s]).start()
            pltpu.make_async_copy(rt.at[side, s], root.at[0, 0, s], out_sem.at[1, side, s]).start()
        return carry

    lax.fori_loop(0, OWN, refresh, 0)

    for i, (a, n) in enumerate(RETURN):
        rows = pl.ds(a, n)
        wait_recv(recv3[i].at[pl.ds(0, OWN * (RANKS - 1))], r3.at[i])
        recv4[i][0] = recv3[i][tab[SLOT3]]

        def step4(k, carry, i=i, rows=rows):
            send4[k, rows, :] = recv3[i][tab[SLOT3 + k]]
            remote(send4.at[k, rows], recv4[i].at[k], s4, r4.at[i], mp_peer(k)).start()
            return carry

        lax.fori_loop(1, GROUPS, step4, 0)

    final = []
    for i, (a, n) in enumerate(RETURN):
        rows = pl.ds(a, n)
        wait_recv(recv4[i].at[pl.ds(1, GROUPS - 1)], r4.at[i])

        def step5(j, carry, i=i, rows=rows):
            outv[j, rows, :] = recv4[i][tab[ORDER4 + j]]
            return carry

        lax.fori_loop(0, GROUPS, step5, 0)
        final.append(pltpu.make_async_copy(outv.at[:, rows, :], out.at[:, rows, :], in_sem.at[i]))
        final[-1].start()

    for s in range(OWN):
        for side, (stat, root) in enumerate(((new_sl, new_rl), (new_sr, new_rr))):
            pltpu.make_async_copy(st.at[side, s], stat.at[0, 0, s], out_sem.at[0, side, s]).wait()
            pltpu.make_async_copy(rt.at[side, s], root.at[0, 0, s], out_sem.at[1, side, s]).wait()
    wait_send(send1.at[pl.ds(1, GROUPS - 1)], s1)
    wait_send(send2.at[pl.ds(0, OWN * (RANKS - 1))], s2)
    wait_send(send3.at[pl.ds(0, OWN * (RANKS - 1))], s3)
    wait_send(send4.at[pl.ds(1, GROUPS - 1)], s4)
    for copy in final:
        copy.wait()


def body(gradient, owner, stat_left, stat_right, root_left, root_right):
    group, rank = lax.axis_index("mp"), lax.axis_index("dp")
    tab = tables(owner, group, rank)
    f32, bf16 = jnp.float32, jnp.bfloat16
    ng, nr = len(GATHER), len(RETURN)
    vmem, dma = pltpu.VMEM, pltpu.SemaphoreType.DMA
    anywhere = pl.BlockSpec(memory_space=pl.ANY)
    scratch = (
        [vmem((GROUPS, n, N), f32) for _, n in GATHER]
        + [vmem((GROUPS, n, N), f32) for _, n in GATHER]
        + [vmem((OWN * RANKS, n, N), f32) for _, n in RETURN]
        + [vmem((GROUPS, n, N), f32) for _, n in RETURN]
        + [
            vmem((GROUPS, ROWS, N), f32),
            vmem((OWN * RANKS, ROWS, N), f32),
            vmem((OWN, RANKS, ROWS, N), f32),
            vmem((OWN * RANKS, ROWS, N), f32),
            vmem((GROUPS, ROWS, N), f32),
            vmem((GROUPS, ROWS, N), f32),
            vmem((2, OWN, N, N), f32),
            vmem((2, OWN, N, N), bf16),
            vmem((2, OWN, 2, N, N), bf16),
        ]
        + [
            dma((max(ng + 4, nr),)),
            dma((2, 2, OWN)),
            dma,
            dma((ng,)),
            dma,
            dma((OWN,)),
            dma,
            dma((nr,)),
            dma,
            dma((nr,)),
        ]
    )
    shape = jax.ShapeDtypeStruct
    return pl.pallas_call(
        kernel,
        out_shape=(
            shape(gradient.shape, f32),
            shape(stat_left.shape, f32),
            shape(stat_right.shape, f32),
            shape(root_left.shape, bf16),
            shape(root_right.shape, bf16),
        ),
        in_specs=[pl.BlockSpec(memory_space=pltpu.SMEM)] + [anywhere] * 5,
        out_specs=(anywhere,) * 5,
        scratch_shapes=scratch,
        compiler_params=pltpu.CompilerParams(
            collective_id=0, has_side_effects=True, vmem_limit_bytes=60 * 2**20
        ),
        cost_estimate=pl.CostEstimate(flops=75 * 2 * N**3, bytes_accessed=22 * 2**20, transcendentals=0),
        name="refresh",
    )(tab, gradient, stat_left, stat_right, root_left, root_right)


def solution(mesh):
    state = P("dp", "mp", None, None, None)
    return jax.shard_map(
        body,
        mesh=mesh,
        in_specs=(P("mp", "dp", None), P(), state, state, state, state),
        out_specs=(P("mp", "dp", None), state, state, state, state),
        check_vma=False,
    )
```

```python
import functools

import jax
import jax.numpy as jnp
from jax import lax
from jax.experimental import pallas as pl
from jax.experimental.pallas import tpu as pltpu
from jax.sharding import PartitionSpec as P

MESH = pl.DeviceIdType.MESH
N = 512
ROWS = 64
OWN = 3
RANKS = 8
GROUPS = 16
SIDE = 4
GATHER = ((0, 8), (8, 8), (16, 8), (24, 8), (32, 16), (48, 16))
RETURN = ((0, 16), (16, 16), (32, 16), (48, 8), (56, 8))
LATE = 4
EARLY = 2
TINY = 2.0**-48

SEND1, SLOT2, SLOT3, RANK3, ORDER4, LIVE = 0, 16, 40, 56, 72, 88


def tables(owner, group, rank):
    table = owner.reshape(GROUPS, GROUPS)
    of_group, of_rank = table % GROUPS, table // GROUPS
    each = jnp.arange(GROUPS, dtype=jnp.int32)

    def away(target, source):
        dz = (target // SIDE - source // SIDE) % SIDE
        dy = (target % SIDE - source % SIDE) % SIDE
        return dz * SIDE + dy

    mine = lax.dynamic_index_in_dim(of_group, group, 0, keepdims=False)
    sent_to = away(mine, group)
    send1 = jnp.sum(jnp.where(sent_to[None, :] == each[:, None], each[None, :], 0), axis=1)
    rank_of = jnp.sum(jnp.where(of_group == group, of_rank, 0), axis=1)
    before = (rank_of[:, None] == rank_of[None, :]) & (each[:, None] > each[None, :])
    slot_of = jnp.sum(before.astype(jnp.int32), axis=1)
    place = rank_of * OWN + slot_of
    came = away(group, each)
    places = jnp.arange(RANKS * OWN, dtype=jnp.int32)
    hit = place[None, :] == places[:, None]
    slot2 = jnp.sum(jnp.where(hit, came[None, :], 0), axis=1)
    goes = away(each, group)
    met = goes[None, :] == each[:, None]
    slot3 = jnp.sum(jnp.where(met, slot_of[None, :], 0), axis=1)
    rank3 = jnp.sum(jnp.where(met, rank_of[None, :], 0), axis=1)
    order4 = away(group, mine)
    slots = jnp.arange(OWN, dtype=jnp.int32)
    live = jnp.any(place[None, :] == (rank * OWN + slots)[:, None], axis=1).astype(jnp.int32)
    return jnp.concatenate([send1, slot2, slot3, rank3, order4, live]).astype(jnp.int32)


def split(x):
    high = x.astype(jnp.bfloat16)
    return high, (x - high.astype(jnp.float32)).astype(jnp.bfloat16)


def dot(a, b):
    return jnp.dot(a, b, preferred_element_type=jnp.float32)


def dot3(a, b):
    (ah, al), (bh, bl) = a, b
    return dot(ah, bh) + (dot(ah, bl) + dot(al, bh))


def kernel(tab, grad, stat_l, stat_r, root_l, root_r, outv, new_sl, new_sr, new_rl, new_rr, *scratch):
    ng, nr = len(GATHER), len(RETURN)
    scratch = list(scratch)
    take = lambda count: [scratch.pop(0) for _ in range(count)]
    staged, recv1, recv3, recv4 = take(ng), take(ng), take(nr), take(nr)
    send1, send2, gbuf, send3, send4, x5 = take(6)
    in_sem, s1, r1, s2, r2, s3, r3, s4, r4 = take(9)

    st, rt = (new_sl.at[0, 0], new_sr.at[0, 0]), (new_rl.at[0, 0], new_rr.at[0, 0])
    rank, group = lax.axis_index("dp"), lax.axis_index("mp")
    z, y = group // SIDE, group % SIDE

    def mp_peer(k):
        return (rank, ((z + k // SIDE) % SIDE) * SIDE + (y + k % SIDE) % SIDE)

    def dp_peer(d):
        return ((rank + d) % RANKS, group)

    def remote(src, dst, ssem, rsem, peer):
        return pltpu.make_async_remote_copy(
            src_ref=src, dst_ref=dst, send_sem=ssem, recv_sem=rsem, device_id=peer, device_id_type=MESH
        )

    def wait_recv(region, sem):
        remote(region, region, s1, sem, dp_peer(1)).wait_recv()

    def wait_send(region, sem):
        remote(region, region, sem, r1.at[0], dp_peer(1)).wait_send()

    grad_in = [
        pltpu.make_async_copy(grad.at[:, pl.ds(a, n), :], staged[i], in_sem.at[i]) for i, (a, n) in enumerate(GATHER)
    ]
    state_in = [
        pltpu.make_async_copy(src.at[0, 0], dst, in_sem.at[ng + i])
        for i, (src, dst) in enumerate(
            ((root_l, rt[0]), (root_r, rt[1]), (stat_l, st[0]), (stat_r, st[1]))
        )
    ]
    for copy in grad_in + state_in:
        copy.start()

    barrier = pltpu.get_barrier_semaphore()

    def greet_mp(k, carry):
        pl.semaphore_signal(barrier, inc=1, device_id=mp_peer(k), device_id_type=MESH)
        return carry

    def greet_dp(d, carry):
        pl.semaphore_signal(barrier, inc=1, device_id=dp_peer(d), device_id_type=MESH)
        return carry

    lax.fori_loop(1, GROUPS, greet_mp, 0)
    lax.fori_loop(1, RANKS, greet_dp, 0)
    pl.semaphore_wait(barrier, GROUPS - 1 + RANKS - 1)

    for i, (a, n) in enumerate(GATHER):
        grad_in[i].wait()
        rows = pl.ds(a, n)
        recv1[i][0] = staged[i][tab[SEND1]]

        def step1(k, carry, i=i, rows=rows):
            send1[k, rows, :] = staged[i][tab[SEND1 + k]]
            remote(send1.at[k, rows], recv1[i].at[k], s1, r1.at[i], mp_peer(k)).start()
            return carry

        lax.fori_loop(1, GROUPS, step1, 0)

    def second(i, slots):
        rows = pl.ds(*GATHER[i])

        def fill(d, carry):
            peer = (rank + d) % RANKS
            for s in range(OWN):
                send2[d, s, rows, :] = recv1[i][tab[SLOT2 + peer * OWN + s]]
            return carry

        def step2(d, carry):
            fill(d, carry)
            leave(d, slots, rows, 0 if slots == OWN else 1)
            return carry

        lax.fori_loop(1, RANKS, step2, 0)

    def leave(d, slots, rows, sem):
        some = pl.ds(0, slots)
        remote(send2.at[d, some, rows], gbuf.at[some, rank, rows], s2, r2.at[sem], dp_peer(d)).start()

    late_from = GATHER[LATE][0]
    late_rows = pl.ds(late_from, ROWS - late_from)

    def step2_late(d, carry):
        some = pl.ds(OWN - 1, 1)
        remote(send2.at[d, some, late_rows], gbuf.at[some, rank, late_rows], s2, r2.at[2], dp_peer(d)).start()
        return carry

    def own_rows(i):
        a, n = GATHER[i]
        for s in range(OWN):
            gbuf[s, rank, pl.ds(a, n), :] = recv1[i][tab[SLOT2 + rank * OWN + s]]

    def power(t):
        side = t % 2
        s = t // 2
        x = rt[side][s]
        sq = split(dot(x, x))
        fourth = split(dot3(sq, sq) * TINY)
        high, low = split(dot(x, fourth[0]) + dot(x, fourth[1]))
        x5[side, s, 0] = high
        x5[side, s, 1] = low

    for i in range(ng):
        wait_recv(recv1[i].at[pl.ds(1, GROUPS - 1)], r1.at[i])
        second(i, OWN if i < LATE else OWN - 1)
        if i == ng - 1:
            lax.fori_loop(1, RANKS, step2_late, 0)
        own_rows(i)
        if i == 0:
            state_in[0].wait()
            state_in[1].wait()
        power(i)
    state_in[2].wait()
    state_in[3].wait()

    eye = lax.broadcasted_iota(jnp.int32, (N, N), 0) == lax.broadcasted_iota(jnp.int32, (N, N), 1)

    def newton(side, s, new, taken):
        scale = jnp.sum(jnp.where(eye, new, 0.0)) / N
        shifted = split(new / scale + jnp.where(eye, 0.001, 0.0))
        moved = dot3((x5[side, s, 0], x5[side, s, 1]), shifted)
        inverse = 1.25 * rt[side][s].astype(jnp.float32) - (0.25 / TINY) * moved
        st[side][s] = jnp.where(taken, new, 0.0)
        rt[side][s] = jnp.where(taken, inverse, 0.0).astype(jnp.bfloat16)
        return inverse

    def refresh(s):
        taken = tab[LIVE + s] > 0
        g32 = gbuf[s].reshape(N, N)
        g, gt = split(g32), split(g32.T)
        inv_l = newton(0, s, 0.95 * st[0][s] + dot3(g, gt), taken)
        inv_r = newton(1, s, 0.95 * st[1][s] + dot3(gt, g), taken)
        result = dot3(split(dot3(split(inv_l), g)), split(inv_r))
        send3[s] = result.reshape(RANKS, ROWS, N)

    def back(i, first, count):
        rows, some = pl.ds(*RETURN[i]), pl.ds(first, count)

        def step3(d, carry):
            peer = (rank + d) % RANKS
            remote(send3.at[some, peer, rows], recv3[i].at[some, rank], s3, r3.at[i], dp_peer(d)).start()
            return carry

        lax.fori_loop(1, RANKS, step3, 0)
        for s in range(first, first + count):
            recv3[i][s, rank] = send3[s, rank, rows, :]

    early = pl.ds(0, late_from)
    wait_recv(gbuf.at[:, pl.ds(0, RANKS - 1), early], r2.at[0])
    wait_recv(gbuf.at[pl.ds(0, OWN - 1), pl.ds(0, RANKS - 1), late_rows], r2.at[1])
    refresh(0)
    for i in range(EARLY):
        back(i, 0, 1)
    lax.fori_loop(1, OWN - 1, lambda s, carry: (refresh(s), carry)[1], 0)
    wait_recv(gbuf.at[pl.ds(OWN - 1, 1), pl.ds(0, RANKS - 1), late_rows], r2.at[2])
    refresh(OWN - 1)
    for i in range(nr):
        back(i, *((1, OWN - 1) if i < EARLY else (0, OWN)))

    for i, (a, n) in enumerate(RETURN):
        rows = pl.ds(a, n)
        wait_recv(recv3[i].at[:, pl.ds(0, RANKS - 1)], r3.at[i])

        def pick(k, i=i):
            return recv3[i][tab[SLOT3 + k], tab[RANK3 + k]]

        recv4[i][0] = pick(0)

        def step4(k, carry, i=i, rows=rows, pick=pick):
            send4[k, rows, :] = pick(k)
            remote(send4.at[k, rows], recv4[i].at[k], s4, r4.at[i], mp_peer(k)).start()
            return carry

        lax.fori_loop(1, GROUPS, step4, 0)

    for i, (a, n) in enumerate(RETURN):
        rows = pl.ds(a, n)
        wait_recv(recv4[i].at[pl.ds(1, GROUPS - 1)], r4.at[i])

        def step5(j, carry, i=i, rows=rows):
            outv[j, rows, :] = recv4[i][tab[ORDER4 + j]]
            return carry

        lax.fori_loop(0, GROUPS, step5, 0)

    wait_send(send1.at[pl.ds(1, GROUPS - 1)], s1)
    wait_send(send2.at[pl.ds(1, RANKS - 1)], s2)
    wait_send(send3.at[:, pl.ds(0, RANKS - 1)], s3)
    wait_send(send4.at[pl.ds(1, GROUPS - 1)], s4)


def finish(*refs):
    count = len(refs) // 2
    copies = [pltpu.make_async_copy(refs[i], refs[count + i], refs[-1].at[i]) for i in range(count)]
    for copy in copies:
        copy.start()
    for copy in copies:
        copy.wait()


def body(gradient, owner, stat_left, stat_right, root_left, root_right):
    group, rank = lax.axis_index("mp"), lax.axis_index("dp")
    tab = tables(owner, group, rank)
    f32, bf16 = jnp.float32, jnp.bfloat16
    ng, nr = len(GATHER), len(RETURN)
    vmem, dma = pltpu.VMEM, pltpu.SemaphoreType.DMA
    anywhere = pl.BlockSpec(memory_space=pl.ANY)
    scratch = (
        [vmem((GROUPS, n, N), f32) for _, n in GATHER]
        + [vmem((GROUPS, n, N), f32) for _, n in GATHER]
        + [vmem((OWN, RANKS, n, N), f32) for _, n in RETURN]
        + [vmem((GROUPS, n, N), f32) for _, n in RETURN]
        + [
            vmem((GROUPS, ROWS, N), f32),
            vmem((RANKS, OWN, ROWS, N), f32),
            vmem((OWN, RANKS, ROWS, N), f32),
            vmem((OWN, RANKS, ROWS, N), f32),
            vmem((GROUPS, ROWS, N), f32),
            vmem((2, OWN, 2, N, N), bf16),
        ]
        + [dma((ng + 4,)), dma, dma((ng,)), dma, dma((3,)), dma, dma((nr,)), dma, dma((nr,))]
    )
    args = (gradient, stat_left, stat_right, root_left, root_right)
    results = pl.pallas_call(
        kernel,
        out_shape=tuple(pltpu.VMEM(x.shape, x.dtype) for x in args),
        in_specs=[pl.BlockSpec(memory_space=pltpu.SMEM)] + [anywhere] * 5,
        out_specs=(pl.BlockSpec(memory_space=pltpu.VMEM),) * 5,
        scratch_shapes=scratch,
        compiler_params=pltpu.CompilerParams(
            collective_id=0, has_side_effects=True, vmem_limit_bytes=48 * 2**20
        ),
        cost_estimate=pl.CostEstimate(flops=75 * 2 * N**3, bytes_accessed=22 * 2**20, transcendentals=0),
        name="refresh",
    )(tab, *args)
    return pl.pallas_call(
        finish,
        out_shape=tuple(jax.ShapeDtypeStruct(x.shape, x.dtype) for x in args),
        in_specs=[anywhere] * 5,
        out_specs=(anywhere,) * 5,
        scratch_shapes=[dma((5,))],
        name="finish",
    )(*results)


def solution(mesh):
    state = P("dp", "mp", None, None, None)
    return jax.shard_map(
        body,
        mesh=mesh,
        in_specs=(P("mp", "dp", None), P(), state, state, state, state),
        out_specs=(P("mp", "dp", None), state, state, state, state),
        check_vma=False,
    )
```

```python
import functools

import jax
import jax.numpy as jnp
from jax import lax
from jax.experimental import pallas as pl
from jax.experimental.pallas import tpu as pltpu
from jax.sharding import PartitionSpec as P

MESH = pl.DeviceIdType.MESH
N = 512
ROWS = 64
OWN = 3
RANKS = 8
GROUPS = 16
SIDE = 4
GATHER = ((0, 8), (8, 8), (16, 8), (24, 8), (32, 16), (48, 16))
RETURN = ((0, 16), (16, 16), (32, 16), (48, 8), (56, 8))
INWARD = (
    (0, 0, 2, 0, 0), (1, 0, 2, 1, 1), (2, 0, 2, 2, 2), (3, 0, 2, 3, 3),
    (4, 0, 1, 4, 4), (5, 0, 0, 5, 5), (5, 1, 1, 5, 5), (5, 2, 2, 4, 5),
)
OUTWARD = (
    (0, 0, 0, 0), (0, 0, 0, 1), (1, 1, 1, 0), (2, 2, 2, 0), (2, 1, 2, 1), (2, 0, 2, 2), (2, 0, 2, 3), (2, 0, 2, 4),
)
AHEAD = 3
TINY = 2.0**-48

SEND1, SLOT2, SLOT3, RANK3, ORDER4, LIVE = 0, 16, 40, 56, 72, 88


def tables(owner, group, rank):
    table = owner.reshape(GROUPS, GROUPS)
    of_group, of_rank = table % GROUPS, table // GROUPS
    each = jnp.arange(GROUPS, dtype=jnp.int32)

    def away(target, source):
        dz = (target // SIDE - source // SIDE) % SIDE
        dy = (target % SIDE - source % SIDE) % SIDE
        return dz * SIDE + dy

    mine = lax.dynamic_index_in_dim(of_group, group, 0, keepdims=False)
    sent_to = away(mine, group)
    send1 = jnp.sum(jnp.where(sent_to[None, :] == each[:, None], each[None, :], 0), axis=1)
    rank_of = jnp.sum(jnp.where(of_group == group, of_rank, 0), axis=1)
    before = (rank_of[:, None] == rank_of[None, :]) & (each[:, None] > each[None, :])
    slot_of = jnp.sum(before.astype(jnp.int32), axis=1)
    place = rank_of * OWN + slot_of
    came = away(group, each)
    places = jnp.arange(RANKS * OWN, dtype=jnp.int32)
    hit = place[None, :] == places[:, None]
    slot2 = jnp.sum(jnp.where(hit, came[None, :], 0), axis=1)
    goes = away(each, group)
    met = goes[None, :] == each[:, None]
    slot3 = jnp.sum(jnp.where(met, slot_of[None, :], 0), axis=1)
    rank3 = jnp.sum(jnp.where(met, rank_of[None, :], 0), axis=1)
    order4 = away(group, mine)
    slots = jnp.arange(OWN, dtype=jnp.int32)
    live = jnp.any(place[None, :] == (rank * OWN + slots)[:, None], axis=1).astype(jnp.int32)
    return jnp.concatenate([send1, slot2, slot3, rank3, order4, live]).astype(jnp.int32)


def split(x):
    high = x.astype(jnp.bfloat16)
    return high, (x - high.astype(jnp.float32)).astype(jnp.bfloat16)


def dot(a, b):
    return jnp.dot(a, b, preferred_element_type=jnp.float32)


def dot3(a, b):
    (ah, al), (bh, bl) = a, b
    return dot(ah, bh) + (dot(ah, bl) + dot(al, bh))


def kernel(tab, grad, stat_l, stat_r, root_l, root_r, outv, new_sl, new_sr, new_rl, new_rr, *scratch):
    ng, nr = len(GATHER), len(RETURN)
    scratch = list(scratch)
    take = lambda count: [scratch.pop(0) for _ in range(count)]
    staged, recv1, recv3, recv4 = take(ng), take(ng), take(nr), take(nr)
    send1, send2, gbuf, send3, send4, x5 = take(6)
    in_sem, s1, r1, s2, r2, s3, r3, s4, r4 = take(9)

    st, rt = (new_sl.at[0, 0], new_sr.at[0, 0]), (new_rl.at[0, 0], new_rr.at[0, 0])
    rank, group = lax.axis_index("dp"), lax.axis_index("mp")
    z, y = group // SIDE, group % SIDE

    def mp_peer(k):
        return (rank, ((z + k // SIDE) % SIDE) * SIDE + (y + k % SIDE) % SIDE)

    def dp_peer(d):
        return ((rank + d) % RANKS, group)

    def remote(src, dst, ssem, rsem, peer):
        return pltpu.make_async_remote_copy(
            src_ref=src, dst_ref=dst, send_sem=ssem, recv_sem=rsem, device_id=peer, device_id_type=MESH
        )

    def wait_recv(region, sem):
        remote(region, region, s1, sem, dp_peer(1)).wait_recv()

    def wait_send(region, sem):
        remote(region, region, sem, r1.at[0], dp_peer(1)).wait_send()

    grad_in = [
        pltpu.make_async_copy(grad.at[:, pl.ds(a, n), :], staged[i], in_sem.at[i]) for i, (a, n) in enumerate(GATHER)
    ]
    state_in = [
        pltpu.make_async_copy(src.at[0, 0], dst, in_sem.at[ng + i])
        for i, (src, dst) in enumerate(
            ((root_l, rt[0]), (root_r, rt[1]), (stat_l, st[0]), (stat_r, st[1]))
        )
    ]
    for copy in grad_in + state_in:
        copy.start()

    barrier = pltpu.get_barrier_semaphore()

    def greet_mp(k, carry):
        pl.semaphore_signal(barrier, inc=1, device_id=mp_peer(k), device_id_type=MESH)
        return carry

    def greet_dp(d, carry):
        pl.semaphore_signal(barrier, inc=1, device_id=dp_peer(d), device_id_type=MESH)
        return carry

    lax.fori_loop(1, GROUPS, greet_mp, 0)
    lax.fori_loop(1, RANKS, greet_dp, 0)
    pl.semaphore_wait(barrier, GROUPS - 1 + RANKS - 1)

    def first(i):
        grad_in[i].wait()
        rows = pl.ds(*GATHER[i])
        recv1[i][0] = staged[i][tab[SEND1]]

        def step1(k, carry):
            send1[k, rows, :] = staged[i][tab[SEND1 + k]]
            remote(send1.at[k, rows], recv1[i].at[k], s1, r1.at[i], mp_peer(k)).start()
            return carry

        lax.fori_loop(1, GROUPS, step1, 0)

    def region(first_chunk, last_chunk):
        start = GATHER[first_chunk][0]
        return pl.ds(start, sum(GATHER[last_chunk]) - start)

    def second(i):
        rows = pl.ds(*GATHER[i])

        def fill(d, carry):
            peer = (rank + d) % RANKS
            for s in range(OWN):
                send2[d, s, rows, :] = recv1[i][tab[SLOT2 + peer * OWN + s]]
            return carry

        for order, (after, first_slot, last_slot, first_chunk, last_chunk) in enumerate(INWARD):
            if after != i:
                continue
            slots, part = pl.ds(first_slot, last_slot - first_slot + 1), region(first_chunk, last_chunk)

            def step2(d, carry, order=order, slots=slots, part=part, filled=fill):
                if filled is not None:
                    filled(d, carry)
                remote(
                    send2.at[d, slots, part], gbuf.at[slots, rank, part], s2, r2.at[order], dp_peer(d)
                ).start()
                return carry

            lax.fori_loop(1, RANKS, step2, 0)
            fill = None

    def own_rows(i):
        a, n = GATHER[i]
        for s in range(OWN):
            gbuf[s, rank, pl.ds(a, n), :] = recv1[i][tab[SLOT2 + rank * OWN + s]]

    def power(t):
        side = t % 2
        s = t // 2
        x = rt[side][s]
        sq = split(dot(x, x))
        fourth = split(dot3(sq, sq) * TINY)
        high, low = split(dot(x, fourth[0]) + dot(x, fourth[1]))
        x5[side, s, 0] = high
        x5[side, s, 1] = low

    for i in range(AHEAD):
        first(i)
    for i in range(ng):
        wait_recv(recv1[i].at[pl.ds(1, GROUPS - 1)], r1.at[i])
        second(i)
        if i + AHEAD < ng:
            first(i + AHEAD)
        own_rows(i)
        if i == 0:
            state_in[0].wait()
            state_in[1].wait()
        power(i)
    state_in[2].wait()
    state_in[3].wait()

    eye = lax.broadcasted_iota(jnp.int32, (N, N), 0) == lax.broadcasted_iota(jnp.int32, (N, N), 1)

    def newton(side, s, new, taken):
        scale = jnp.sum(jnp.where(eye, new, 0.0)) / N
        shifted = split(new / scale + jnp.where(eye, 0.001, 0.0))
        moved = dot3((x5[side, s, 0], x5[side, s, 1]), shifted)
        inverse = 1.25 * rt[side][s].astype(jnp.float32) - (0.25 / TINY) * moved
        st[side][s] = jnp.where(taken, new, 0.0)
        rt[side][s] = jnp.where(taken, inverse, 0.0).astype(jnp.bfloat16)
        return inverse

    def refresh(s):
        taken = tab[LIVE + s] > 0
        g32 = gbuf[s].reshape(N, N)
        g, gt = split(g32), split(g32.T)
        inv_l = newton(0, s, 0.95 * st[0][s] + dot3(g, gt), taken)
        inv_r = newton(1, s, 0.95 * st[1][s] + dot3(gt, g), taken)
        result = dot3(split(dot3(split(inv_l), g)), split(inv_r))
        send3[s] = result.reshape(RANKS, ROWS, N)

    def back(i, first, count):
        rows, some = pl.ds(*RETURN[i]), pl.ds(first, count)

        def step3(d, carry):
            peer = (rank + d) % RANKS
            remote(send3.at[some, peer, rows], recv3[i].at[some, rank], s3, r3.at[i], dp_peer(d)).start()
            return carry

        lax.fori_loop(1, RANKS, step3, 0)
        for s in range(first, first + count):
            recv3[i][s, rank] = send3[s, rank, rows, :]

    waited = set()
    for s in range(OWN):
        for order, (_, first_slot, last_slot, first_chunk, last_chunk) in enumerate(INWARD):
            if first_slot <= s <= last_slot and order not in waited:
                waited.add(order)
                slots = pl.ds(first_slot, last_slot - first_slot + 1)
                wait_recv(gbuf.at[slots, pl.ds(0, RANKS - 1), region(first_chunk, last_chunk)], r2.at[order])
        refresh(s)
        for after, first_slot, last_slot, chunk in OUTWARD:
            if after == s:
                back(chunk, first_slot, last_slot - first_slot + 1)

    for i, (a, n) in enumerate(RETURN):
        rows = pl.ds(a, n)
        wait_recv(recv3[i].at[:, pl.ds(0, RANKS - 1)], r3.at[i])

        def pick(k, i=i):
            return recv3[i][tab[SLOT3 + k], tab[RANK3 + k]]

        recv4[i][0] = pick(0)

        def step4(k, carry, i=i, rows=rows, pick=pick):
            send4[k, rows, :] = pick(k)
            remote(send4.at[k, rows], recv4[i].at[k], s4, r4.at[i], mp_peer(k)).start()
            return carry

        lax.fori_loop(1, GROUPS, step4, 0)

    for i, (a, n) in enumerate(RETURN):
        rows = pl.ds(a, n)
        wait_recv(recv4[i].at[pl.ds(1, GROUPS - 1)], r4.at[i])

        def step5(j, carry, i=i, rows=rows):
            outv[j, rows, :] = recv4[i][tab[ORDER4 + j]]
            return carry

        lax.fori_loop(0, GROUPS, step5, 0)

    wait_send(send1.at[pl.ds(1, GROUPS - 1)], s1)
    wait_send(send2.at[pl.ds(1, RANKS - 1)], s2)
    wait_send(send3.at[:, pl.ds(0, RANKS - 1)], s3)
    wait_send(send4.at[pl.ds(1, GROUPS - 1)], s4)


def finish(*refs):
    count = len(refs) // 2
    copies = [pltpu.make_async_copy(refs[i], refs[count + i], refs[-1].at[i]) for i in range(count)]
    for copy in copies:
        copy.start()
    for copy in copies:
        copy.wait()


def body(gradient, owner, stat_left, stat_right, root_left, root_right):
    group, rank = lax.axis_index("mp"), lax.axis_index("dp")
    tab = tables(owner, group, rank)
    f32, bf16 = jnp.float32, jnp.bfloat16
    ng, nr = len(GATHER), len(RETURN)
    vmem, dma = pltpu.VMEM, pltpu.SemaphoreType.DMA
    anywhere = pl.BlockSpec(memory_space=pl.ANY)
    scratch = (
        [vmem((GROUPS, n, N), f32) for _, n in GATHER]
        + [vmem((GROUPS, n, N), f32) for _, n in GATHER]
        + [vmem((OWN, RANKS, n, N), f32) for _, n in RETURN]
        + [vmem((GROUPS, n, N), f32) for _, n in RETURN]
        + [
            vmem((GROUPS, ROWS, N), f32),
            vmem((RANKS, OWN, ROWS, N), f32),
            vmem((OWN, RANKS, ROWS, N), f32),
            vmem((OWN, RANKS, ROWS, N), f32),
            vmem((GROUPS, ROWS, N), f32),
            vmem((2, OWN, 2, N, N), bf16),
        ]
        + [dma((ng + 4,)), dma, dma((ng,)), dma, dma((len(INWARD),)), dma, dma((nr,)), dma, dma((nr,))]
    )
    args = (gradient, stat_left, stat_right, root_left, root_right)
    results = pl.pallas_call(
        kernel,
        out_shape=tuple(pltpu.VMEM(x.shape, x.dtype) for x in args),
        in_specs=[pl.BlockSpec(memory_space=pltpu.SMEM)] + [anywhere] * 5,
        out_specs=(pl.BlockSpec(memory_space=pltpu.VMEM),) * 5,
        scratch_shapes=scratch,
        compiler_params=pltpu.CompilerParams(
            collective_id=0, has_side_effects=True, vmem_limit_bytes=48 * 2**20
        ),
        cost_estimate=pl.CostEstimate(flops=75 * 2 * N**3, bytes_accessed=22 * 2**20, transcendentals=0),
        name="refresh",
    )(tab, *args)
    return pl.pallas_call(
        finish,
        out_shape=tuple(jax.ShapeDtypeStruct(x.shape, x.dtype) for x in args),
        in_specs=[pl.BlockSpec(memory_space=pltpu.VMEM)] * 5,
        out_specs=(anywhere,) * 5,
        scratch_shapes=[dma((5,))],
        compiler_params=pltpu.CompilerParams(vmem_limit_bytes=4 * 2**20),
        name="finish",
    )(*[pltpu.with_memory_space_constraint(x, pltpu.VMEM) for x in results])


def solution(mesh):
    state = P("dp", "mp", None, None, None)
    return jax.shard_map(
        body,
        mesh=mesh,
        in_specs=(P("mp", "dp", None), P(), state, state, state, state),
        out_specs=(P("mp", "dp", None), state, state, state, state),
        check_vma=False,
    )
```

```python
import functools

import jax
import jax.numpy as jnp
from jax import lax
from jax.experimental import pallas as pl
from jax.experimental.pallas import tpu as pltpu
from jax.sharding import PartitionSpec as P

MESH = pl.DeviceIdType.MESH
N = 512
ROWS = 64
OWN = 3
RANKS = 8
GROUPS = 16
SIDE = 4
GATHER = ((0, 8), (8, 8), (16, 8), (24, 8), (32, 16), (48, 16))
RETURN = ((0, 16), (16, 16), (32, 16), (48, 8), (56, 8))
INWARD = (
    (0, 0, 2, 0, 0), (1, 0, 2, 1, 1), (2, 0, 2, 2, 2), (3, 0, 2, 3, 3),
    (4, 0, 1, 4, 4), (5, 0, 0, 5, 5), (5, 1, 1, 5, 5), (5, 2, 2, 4, 5),
)
PARTS = (((0, 64),), ((0, 64),), ((0, 16), (16, 48)))
OUTWARD = (
    (0, 0, 0, 0, 0), (0, 0, 0, 0, 1), (1, 0, 1, 1, 0), (2, 0, 2, 2, 0),
    (2, 1, 1, 2, 1), (2, 1, 0, 2, 2), (2, 1, 0, 2, 3), (2, 1, 0, 2, 4),
)
AHEAD = 3
TINY = 2.0**-48

SLOTS = OWN * RANKS
SEND1, RANK_OF, SLOT_OF, SLOT2, LIVE = 0, GROUPS, 2 * GROUPS, 3 * GROUPS, 3 * GROUPS + SLOTS


def away(target, source):
    dz = lax.rem(lax.div(target, SIDE) - lax.div(source, SIDE) + SIDE, SIDE)
    dy = lax.rem(lax.rem(target, SIDE) - lax.rem(source, SIDE) + SIDE, SIDE)
    return dz * SIDE + dy


def within(index, size):
    return jnp.minimum(jnp.maximum(index, 0), size - 1)


def total(terms):
    return functools.reduce(lambda x, y: x + y, terms)


def split(x):
    high = x.astype(jnp.bfloat16)
    return high, (x - high.astype(jnp.float32)).astype(jnp.bfloat16)


def dot(a, b):
    return jnp.dot(a, b, preferred_element_type=jnp.float32)


def dot3(a, b):
    (ah, al), (bh, bl) = a, b
    return dot(ah, bh) + (dot(ah, bl) + dot(al, bh))


def kernel(owner, grad, stat_l, stat_r, root_l, root_r, outv, new_sl, new_sr, new_rl, new_rr, *scratch):
    ng, nr = len(GATHER), len(RETURN)
    scratch = list(scratch)
    take = lambda count: [scratch.pop(0) for _ in range(count)]
    staged, recv1, recv3, recv4 = take(ng), take(ng), take(nr), take(nr)
    send1, send2, gbuf, send3, send4, x5 = take(6)
    in_sem, s1, r1, s2, r2, s3, r3, s4, r4, tab = take(10)

    st, rt = (new_sl.at[0, 0], new_sr.at[0, 0]), (new_rl.at[0, 0], new_rr.at[0, 0])
    rank, group = lax.axis_index("dp"), lax.axis_index("mp")
    z, y = group // SIDE, group % SIDE

    def mp_peer(k):
        return (rank, ((z + k // SIDE) % SIDE) * SIDE + (y + k % SIDE) % SIDE)

    def dp_peer(d):
        return ((rank + d) % RANKS, group)

    def remote(src, dst, ssem, rsem, peer):
        return pltpu.make_async_remote_copy(
            src_ref=src, dst_ref=dst, send_sem=ssem, recv_sem=rsem, device_id=peer, device_id_type=MESH
        )

    def wait_recv(region, sem):
        remote(region, region, s1, sem, dp_peer(1)).wait_recv()

    def wait_send(region, sem):
        remote(region, region, sem, r1.at[0], dp_peer(1)).wait_send()

    grad_in = [
        pltpu.make_async_copy(grad.at[:, pl.ds(a, n), :], staged[i], in_sem.at[i]) for i, (a, n) in enumerate(GATHER)
    ]
    state_in = [
        pltpu.make_async_copy(src.at[0, 0], dst, in_sem.at[ng + i])
        for i, (src, dst) in enumerate(
            ((root_l, rt[0]), (root_r, rt[1]), (stat_l, st[0]), (stat_r, st[1]))
        )
    ]
    for copy in grad_in + state_in:
        copy.start()

    def choose_first(k, carry):
        target = mp_peer(k)[1]
        tab[SEND1 + k] = total(
            jnp.where(lax.rem(owner[group * GROUPS + j], GROUPS) == target, j, 0) for j in range(GROUPS)
        )
        return carry

    def choose_rank(g, carry):
        here = [owner[g * GROUPS + j] for j in range(GROUPS)]
        tab[RANK_OF + g] = total(jnp.where(lax.rem(o, GROUPS) == group, lax.div(o, GROUPS), 0) for o in here)
        return carry

    def choose_slot(g, carry):
        mine = tab[RANK_OF + g]
        tab[SLOT_OF + g] = total(
            jnp.where((tab[RANK_OF + c] == mine) & (c < g), 1, 0) for c in range(GROUPS)
        )
        return carry

    def choose_second(p, carry):
        places = [tab[RANK_OF + g] * OWN + tab[SLOT_OF + g] for g in range(GROUPS)]
        tab[SLOT2 + p] = total(jnp.where(places[g] == p, away(group, g), 0) for g in range(GROUPS))
        tab[LIVE + p] = total(jnp.where(places[g] == p, 1, 0) for g in range(GROUPS))
        return carry

    barrier = pltpu.get_barrier_semaphore()

    def greet_mp(k, carry):
        pl.semaphore_signal(barrier, inc=1, device_id=mp_peer(k), device_id_type=MESH)
        return carry

    def greet_dp(d, carry):
        pl.semaphore_signal(barrier, inc=1, device_id=dp_peer(d), device_id_type=MESH)
        return carry

    lax.fori_loop(1, GROUPS, greet_mp, 0)
    lax.fori_loop(1, RANKS, greet_dp, 0)
    lax.fori_loop(0, GROUPS, choose_first, 0)
    pl.semaphore_wait(barrier, GROUPS - 1 + RANKS - 1)

    def first(i):
        grad_in[i].wait()
        rows = pl.ds(*GATHER[i])
        recv1[i][0] = staged[i][within(tab[SEND1], GROUPS)]

        def step1(k, carry):
            send1[k, rows, :] = staged[i][within(tab[SEND1 + k], GROUPS)]
            remote(send1.at[k, rows], recv1[i].at[k], s1, r1.at[i], mp_peer(k)).start()
            return carry

        lax.fori_loop(1, GROUPS, step1, 0)

    def region(first_chunk, last_chunk):
        start = GATHER[first_chunk][0]
        return pl.ds(start, sum(GATHER[last_chunk]) - start)

    def second(i):
        rows = pl.ds(*GATHER[i])

        def fill(d, carry):
            peer = (rank + d) % RANKS
            for s in range(OWN):
                send2[d, s, rows, :] = recv1[i][within(tab[SLOT2 + peer * OWN + s], GROUPS)]
            return carry

        for order, (after, first_slot, last_slot, first_chunk, last_chunk) in enumerate(INWARD):
            if after != i:
                continue
            slots, part = pl.ds(first_slot, last_slot - first_slot + 1), region(first_chunk, last_chunk)

            def step2(d, carry, order=order, slots=slots, part=part, filled=fill):
                if filled is not None:
                    filled(d, carry)
                remote(
                    send2.at[d, slots, part], gbuf.at[slots, rank, part], s2, r2.at[order], dp_peer(d)
                ).start()
                return carry

            lax.fori_loop(1, RANKS, step2, 0)
            fill = None

    def own_rows(i):
        a, n = GATHER[i]
        for s in range(OWN):
            gbuf[s, rank, pl.ds(a, n), :] = recv1[i][within(tab[SLOT2 + rank * OWN + s], GROUPS)]

    def power(t):
        side = t % 2
        s = t // 2
        x = rt[side][s]
        sq = split(dot(x, x))
        fourth = split(dot3(sq, sq) * TINY)
        high, low = split(dot(x, fourth[0]) + dot(x, fourth[1]))
        x5[side, s, 0] = high
        x5[side, s, 1] = low

    for i in range(AHEAD):
        first(i)
    lax.fori_loop(0, GROUPS, choose_rank, 0)
    lax.fori_loop(0, GROUPS, choose_slot, 0)
    lax.fori_loop(0, SLOTS, choose_second, 0)
    for i in range(ng):
        wait_recv(recv1[i].at[pl.ds(1, GROUPS - 1)], r1.at[i])
        second(i)
        if i + AHEAD < ng:
            first(i + AHEAD)
        own_rows(i)
        if i == 0:
            state_in[0].wait()
            state_in[1].wait()
        power(i)
    state_in[2].wait()
    state_in[3].wait()

    eye = lax.broadcasted_iota(jnp.int32, (N, N), 0) == lax.broadcasted_iota(jnp.int32, (N, N), 1)

    def shift(side, s, new, taken):
        scale = jnp.sum(jnp.where(eye, new, 0.0)) / N
        st[side][s] = jnp.where(taken, new, 0.0)
        return split(new / scale + jnp.where(eye, 0.001, 0.0))

    def rows_of(x, part):
        return x.reshape(RANKS, ROWS, N)[:, part[0] : sum(part)].reshape(RANKS * part[1], N)

    def newton(side, s, shifted, taken, part):
        high, low = (rows_of(x5[side, s, i], part) for i in range(2))
        moved = dot3((high, low), shifted)
        inverse = 1.25 * rows_of(rt[side][s], part).astype(jnp.float32) - (0.25 / TINY) * moved
        kept = jnp.where(taken, inverse, 0.0).astype(jnp.bfloat16)
        if part == (0, ROWS):
            rt[side][s] = kept
        else:
            for e in range(RANKS):
                rt[side][s, pl.ds(e * ROWS + part[0], part[1]), :] = kept[e * part[1] : (e + 1) * part[1]]
        return split(inverse)

    def refresh(s):
        taken = tab[LIVE + rank * OWN + s] > 0
        g32 = gbuf[s].reshape(N, N)
        g, gt = split(g32), split(g32.T)
        shifted_r = shift(1, s, 0.95 * st[1][s] + dot3(gt, g), taken)
        inv_r = newton(1, s, shifted_r, taken, (0, ROWS))
        shifted_l = shift(0, s, 0.95 * st[0][s] + dot3(g, gt), taken)
        for p, part in enumerate(PARTS[s]):
            inv_l = newton(0, s, shifted_l, taken, part)
            result = dot3(split(dot3(inv_l, g)), inv_r)
            send3[s, :, pl.ds(*part), :] = result.reshape(RANKS, part[1], N)
            for after, after_part, first_slot, last_slot, chunk in OUTWARD:
                if (after, after_part) == (s, p):
                    back(chunk, first_slot, last_slot - first_slot + 1)

    def back(i, first, count):
        rows, some = pl.ds(*RETURN[i]), pl.ds(first, count)

        def step3(d, carry):
            peer = (rank + d) % RANKS
            remote(send3.at[some, peer, rows], recv3[i].at[some, rank], s3, r3.at[i], dp_peer(d)).start()
            return carry

        lax.fori_loop(1, RANKS, step3, 0)
        for s in range(first, first + count):
            recv3[i][s, rank] = send3[s, rank, rows, :]

    waited = set()
    for s in range(OWN):
        for order, (_, first_slot, last_slot, first_chunk, last_chunk) in enumerate(INWARD):
            if first_slot <= s <= last_slot and order not in waited:
                waited.add(order)
                slots = pl.ds(first_slot, last_slot - first_slot + 1)
                wait_recv(gbuf.at[slots, pl.ds(0, RANKS - 1), region(first_chunk, last_chunk)], r2.at[order])
        refresh(s)

    for i, (a, n) in enumerate(RETURN):
        rows = pl.ds(a, n)
        wait_recv(recv3[i].at[:, pl.ds(0, RANKS - 1)], r3.at[i])

        def pick(k, i=i):
            g = mp_peer(k)[1]
            return recv3[i][within(tab[SLOT_OF + g], OWN), within(tab[RANK_OF + g], RANKS)]

        recv4[i][0] = pick(0)

        def step4(k, carry, i=i, rows=rows, pick=pick):
            send4[k, rows, :] = pick(k)
            remote(send4.at[k, rows], recv4[i].at[k], s4, r4.at[i], mp_peer(k)).start()
            return carry

        lax.fori_loop(1, GROUPS, step4, 0)

    for i, (a, n) in enumerate(RETURN):
        rows = pl.ds(a, n)
        wait_recv(recv4[i].at[pl.ds(1, GROUPS - 1)], r4.at[i])

        def step5(j, carry, i=i, rows=rows):
            source = away(group, lax.rem(owner[group * GROUPS + j], GROUPS))
            outv[j, rows, :] = recv4[i][within(source, GROUPS)]
            return carry

        lax.fori_loop(0, GROUPS, step5, 0)

    wait_send(send1.at[pl.ds(1, GROUPS - 1)], s1)
    wait_send(send2.at[pl.ds(1, RANKS - 1)], s2)
    wait_send(send3.at[:, pl.ds(0, RANKS - 1)], s3)
    wait_send(send4.at[pl.ds(1, GROUPS - 1)], s4)


def finish(*refs):
    count = len(refs) // 2
    copies = [pltpu.make_async_copy(refs[i], refs[count + i], refs[-1].at[i]) for i in range(count)]
    for copy in copies:
        copy.start()
    for copy in copies:
        copy.wait()


def body(gradient, owner, stat_left, stat_right, root_left, root_right):
    f32, bf16 = jnp.float32, jnp.bfloat16
    ng, nr = len(GATHER), len(RETURN)
    vmem, dma = pltpu.VMEM, pltpu.SemaphoreType.DMA
    anywhere = pl.BlockSpec(memory_space=pl.ANY)
    scratch = (
        [vmem((GROUPS, n, N), f32) for _, n in GATHER]
        + [vmem((GROUPS, n, N), f32) for _, n in GATHER]
        + [vmem((OWN, RANKS, n, N), f32) for _, n in RETURN]
        + [vmem((GROUPS, n, N), f32) for _, n in RETURN]
        + [
            vmem((GROUPS, ROWS, N), f32),
            vmem((RANKS, OWN, ROWS, N), f32),
            vmem((OWN, RANKS, ROWS, N), f32),
            vmem((OWN, RANKS, ROWS, N), f32),
            vmem((GROUPS, ROWS, N), f32),
            vmem((2, OWN, 2, N, N), bf16),
        ]
        + [dma((ng + 4,)), dma, dma((ng,)), dma, dma((len(INWARD),)), dma, dma((nr,)), dma, dma((nr,)), pltpu.SMEM((LIVE + SLOTS,), jnp.int32)]
    )
    args = (gradient, stat_left, stat_right, root_left, root_right)
    results = pl.pallas_call(
        kernel,
        out_shape=tuple(pltpu.VMEM(x.shape, x.dtype) for x in args),
        in_specs=[pl.BlockSpec(memory_space=pltpu.SMEM)] + [anywhere] * 5,
        out_specs=(pl.BlockSpec(memory_space=pltpu.VMEM),) * 5,
        scratch_shapes=scratch,
        compiler_params=pltpu.CompilerParams(
            collective_id=0, has_side_effects=True, vmem_limit_bytes=48 * 2**20
        ),
        cost_estimate=pl.CostEstimate(flops=75 * 2 * N**3, bytes_accessed=22 * 2**20, transcendentals=0),
        name="refresh",
    )(owner, *args)
    return pl.pallas_call(
        finish,
        out_shape=tuple(jax.ShapeDtypeStruct(x.shape, x.dtype) for x in args),
        in_specs=[pl.BlockSpec(memory_space=pltpu.VMEM)] * 5,
        out_specs=(anywhere,) * 5,
        scratch_shapes=[dma((5,))],
        compiler_params=pltpu.CompilerParams(vmem_limit_bytes=4 * 2**20),
        name="finish",
    )(*[pltpu.with_memory_space_constraint(x, pltpu.VMEM) for x in results])


def solution(mesh):
    state = P("dp", "mp", None, None, None)
    return jax.shard_map(
        body,
        mesh=mesh,
        in_specs=(P("mp", "dp", None), P(), state, state, state, state),
        out_specs=(P("mp", "dp", None), state, state, state, state),
        check_vma=False,
    )
```

```python
import functools

import jax
import jax.numpy as jnp
from jax import lax
from jax.experimental import pallas as pl
from jax.experimental.pallas import tpu as pltpu
from jax.sharding import PartitionSpec as P

MESH = pl.DeviceIdType.MESH
N = 512
ROWS = 64
OWN = 3
RANKS = 8
GROUPS = 16
SIDE = 4
GATHER = (
    (0, 8, 0, 256), (0, 8, 256, 256), (8, 8, 0, N), (16, 8, 0, N), (24, 8, 0, N), (32, 16, 0, N), (48, 16, 0, N),
)
RETURN = ((0, 16, 0, N), (16, 16, 0, N), (32, 16, 0, N), (48, 8, 0, N), (56, 8, 0, 256), (56, 8, 256, 256))
INWARD = (
    (0, 0, 2, 0, 0), (1, 0, 2, 1, 1), (2, 0, 2, 2, 2), (3, 0, 2, 3, 3), (4, 0, 2, 4, 4),
    (5, 0, 1, 5, 5), (6, 0, 0, 6, 6), (6, 1, 1, 6, 6), (6, 2, 2, 5, 6),
)
PARTS = (((0, 64),), ((0, 64),), ((0, 16), (16, 48)))
OUTWARD = (
    (0, 0, 0, 0, 0), (0, 0, 0, 0, 1), (1, 0, 1, 1, 0), (1, 0, 1, 1, 1), (2, 0, 2, 2, 0),
    (2, 1, 2, 2, 1), (2, 1, 0, 2, 2), (2, 1, 0, 2, 3), (2, 1, 0, 2, 4), (2, 1, 0, 2, 5),
)
AHEAD = 4
TINY = 2.0**-48

SLOTS = OWN * RANKS
SEND1, RANK_OF, SLOT_OF, SLOT2, LIVE = 0, GROUPS, 2 * GROUPS, 3 * GROUPS, 3 * GROUPS + SLOTS


def away(target, source):
    dz = lax.rem(lax.div(target, SIDE) - lax.div(source, SIDE) + SIDE, SIDE)
    dy = lax.rem(lax.rem(target, SIDE) - lax.rem(source, SIDE) + SIDE, SIDE)
    return dz * SIDE + dy


def within(index, size):
    return jnp.minimum(jnp.maximum(index, 0), size - 1)


def total(terms):
    return functools.reduce(lambda x, y: x + y, terms)


def cut(chunk):
    return pl.ds(chunk[0], chunk[1]), pl.ds(chunk[2], chunk[3])


def split(x):
    high = x.astype(jnp.bfloat16)
    return high, (x - high.astype(jnp.float32)).astype(jnp.bfloat16)


def dot(a, b):
    return jnp.dot(a, b, preferred_element_type=jnp.float32)


def dot3(a, b):
    (ah, al), (bh, bl) = a, b
    return dot(ah, bh) + (dot(ah, bl) + dot(al, bh))


def kernel(owner, grad, stat_l, stat_r, root_l, root_r, outv, new_sl, new_sr, new_rl, new_rr, *scratch):
    ng, nr = len(GATHER), len(RETURN)
    scratch = list(scratch)
    take = lambda count: [scratch.pop(0) for _ in range(count)]
    staged, recv1, recv3, recv4 = take(ng), take(ng), take(nr), take(nr)
    send1, send2, gbuf, send3, send4, x5 = take(6)
    in_sem, s1, r1, s2, r2, s3, r3, s4, r4, tab = take(10)

    st, rt = (new_sl.at[0, 0], new_sr.at[0, 0]), (new_rl.at[0, 0], new_rr.at[0, 0])
    rank, group = lax.axis_index("dp"), lax.axis_index("mp")
    z, y = group // SIDE, group % SIDE

    def mp_peer(k):
        return (rank, ((z + k // SIDE) % SIDE) * SIDE + (y + k % SIDE) % SIDE)

    def dp_peer(d):
        return ((rank + d) % RANKS, group)

    def remote(src, dst, ssem, rsem, peer):
        return pltpu.make_async_remote_copy(
            src_ref=src, dst_ref=dst, send_sem=ssem, recv_sem=rsem, device_id=peer, device_id_type=MESH
        )

    def wait_recv(region, sem):
        remote(region, region, s1, sem, dp_peer(1)).wait_recv()

    def wait_send(region, sem):
        remote(region, region, sem, r1.at[0], dp_peer(1)).wait_send()

    grad_in = [
        pltpu.make_async_copy(grad.at[:, *cut(chunk)], staged[i], in_sem.at[i]) for i, chunk in enumerate(GATHER)
    ]
    state_in = [
        pltpu.make_async_copy(src.at[0, 0], dst, in_sem.at[ng + i])
        for i, (src, dst) in enumerate(
            ((root_l, rt[0]), (root_r, rt[1]), (stat_l, st[0]), (stat_r, st[1]))
        )
    ]
    for copy in grad_in + state_in:
        copy.start()

    def choose_first(k, carry):
        target = mp_peer(k)[1]
        tab[SEND1 + k] = total(
            jnp.where(lax.rem(owner[group * GROUPS + j], GROUPS) == target, j, 0) for j in range(GROUPS)
        )
        return carry

    def choose_rank(g, carry):
        here = [owner[g * GROUPS + j] for j in range(GROUPS)]
        tab[RANK_OF + g] = total(jnp.where(lax.rem(o, GROUPS) == group, lax.div(o, GROUPS), 0) for o in here)
        return carry

    def choose_slot(g, carry):
        mine = tab[RANK_OF + g]
        tab[SLOT_OF + g] = total(
            jnp.where((tab[RANK_OF + c] == mine) & (c < g), 1, 0) for c in range(GROUPS)
        )
        return carry

    def choose_second(p, carry):
        places = [tab[RANK_OF + g] * OWN + tab[SLOT_OF + g] for g in range(GROUPS)]
        tab[SLOT2 + p] = total(jnp.where(places[g] == p, away(group, g), 0) for g in range(GROUPS))
        tab[LIVE + p] = total(jnp.where(places[g] == p, 1, 0) for g in range(GROUPS))
        return carry

    barrier = pltpu.get_barrier_semaphore()

    def greet_mp(k, carry):
        pl.semaphore_signal(barrier, inc=1, device_id=mp_peer(k), device_id_type=MESH)
        return carry

    def greet_dp(d, carry):
        pl.semaphore_signal(barrier, inc=1, device_id=dp_peer(d), device_id_type=MESH)
        return carry

    lax.fori_loop(1, GROUPS, greet_mp, 0)
    lax.fori_loop(1, RANKS, greet_dp, 0)
    lax.fori_loop(0, GROUPS, choose_first, 0)
    pl.semaphore_wait(barrier, GROUPS - 1 + RANKS - 1)

    def first(i):
        grad_in[i].wait()
        rows, columns = cut(GATHER[i])
        recv1[i][0] = staged[i][within(tab[SEND1], GROUPS)]

        def step1(k, carry):
            send1[k, rows, columns] = staged[i][within(tab[SEND1 + k], GROUPS)]
            remote(send1.at[k, rows, columns], recv1[i].at[k], s1, r1.at[i], mp_peer(k)).start()
            return carry

        lax.fori_loop(1, GROUPS, step1, 0)

    def region(first_chunk, last_chunk):
        start = GATHER[first_chunk][0]
        end = GATHER[last_chunk][0] + GATHER[last_chunk][1]
        columns = GATHER[first_chunk][2:] if first_chunk == last_chunk else (0, N)
        return cut((start, end - start, *columns))

    def second(i):
        rows, columns = cut(GATHER[i])

        def fill(d, carry):
            peer = (rank + d) % RANKS
            for s in range(OWN):
                send2[d, s, rows, columns] = recv1[i][within(tab[SLOT2 + peer * OWN + s], GROUPS)]
            return carry

        for order, (after, first_slot, last_slot, first_chunk, last_chunk) in enumerate(INWARD):
            if after != i:
                continue
            slots, part = pl.ds(first_slot, last_slot - first_slot + 1), region(first_chunk, last_chunk)

            def step2(d, carry, order=order, slots=slots, part=part, filled=fill):
                if filled is not None:
                    filled(d, carry)
                remote(
                    send2.at[d, slots, *part], gbuf.at[slots, rank, *part], s2, r2.at[order], dp_peer(d)
                ).start()
                return carry

            lax.fori_loop(1, RANKS, step2, 0)
            fill = None

    def own_rows(i):
        rows, columns = cut(GATHER[i])
        for s in range(OWN):
            gbuf[s, rank, rows, columns] = recv1[i][within(tab[SLOT2 + rank * OWN + s], GROUPS)]

    def power(t):
        side = t % 2
        s = t // 2
        x = rt[side][s]
        sq = split(dot(x, x))
        fourth = split(dot3(sq, sq) * TINY)
        high, low = split(dot(x, fourth[0]) + dot(x, fourth[1]))
        x5[side, s, 0] = high
        x5[side, s, 1] = low

    for i in range(AHEAD):
        first(i)
    lax.fori_loop(0, GROUPS, choose_rank, 0)
    lax.fori_loop(0, GROUPS, choose_slot, 0)
    lax.fori_loop(0, SLOTS, choose_second, 0)
    for i in range(ng):
        wait_recv(recv1[i].at[pl.ds(1, GROUPS - 1)], r1.at[i])
        second(i)
        if i + AHEAD < ng:
            first(i + AHEAD)
        own_rows(i)
        if i == 0:
            state_in[0].wait()
            state_in[1].wait()
        if i >= ng - 2 * OWN:
            power(i - (ng - 2 * OWN))
    state_in[2].wait()
    state_in[3].wait()

    eye = lax.broadcasted_iota(jnp.int32, (N, N), 0) == lax.broadcasted_iota(jnp.int32, (N, N), 1)

    def shift(side, s, new, taken):
        scale = jnp.sum(jnp.where(eye, new, 0.0)) / N
        st[side][s] = jnp.where(taken, new, 0.0)
        return split(new / scale + jnp.where(eye, 0.001, 0.0))

    def rows_of(x, part):
        return x.reshape(RANKS, ROWS, N)[:, part[0] : sum(part)].reshape(RANKS * part[1], N)

    def newton(side, s, shifted, taken, part):
        high, low = (rows_of(x5[side, s, i], part) for i in range(2))
        moved = dot3((high, low), shifted)
        inverse = 1.25 * rows_of(rt[side][s], part).astype(jnp.float32) - (0.25 / TINY) * moved
        kept = jnp.where(taken, inverse, 0.0).astype(jnp.bfloat16)
        if part == (0, ROWS):
            rt[side][s] = kept
        else:
            for e in range(RANKS):
                rt[side][s, pl.ds(e * ROWS + part[0], part[1]), :] = kept[e * part[1] : (e + 1) * part[1]]
        return split(inverse)

    def refresh(s):
        taken = tab[LIVE + rank * OWN + s] > 0
        g32 = gbuf[s].reshape(N, N)
        g, gt = split(g32), split(g32.T)
        shifted_r = shift(1, s, 0.95 * st[1][s] + dot3(gt, g), taken)
        inv_r = newton(1, s, shifted_r, taken, (0, ROWS))
        shifted_l = shift(0, s, 0.95 * st[0][s] + dot3(g, gt), taken)
        for p, part in enumerate(PARTS[s]):
            inv_l = newton(0, s, shifted_l, taken, part)
            result = dot3(split(dot3(inv_l, g)), inv_r)
            send3[s, :, pl.ds(*part), :] = result.reshape(RANKS, part[1], N)
            for after, after_part, first_slot, last_slot, chunk in OUTWARD:
                if (after, after_part) == (s, p):
                    back(chunk, first_slot, last_slot - first_slot + 1)

    def back(i, first, count):
        (rows, columns), some = cut(RETURN[i]), pl.ds(first, count)

        def step3(d, carry):
            peer = (rank + d) % RANKS
            remote(send3.at[some, peer, rows, columns], recv3[i].at[some, rank], s3, r3.at[i], dp_peer(d)).start()
            return carry

        lax.fori_loop(1, RANKS, step3, 0)
        for s in range(first, first + count):
            recv3[i][s, rank] = send3[s, rank, rows, columns]

    waited = set()
    for s in range(OWN):
        for order, (_, first_slot, last_slot, first_chunk, last_chunk) in enumerate(INWARD):
            if first_slot <= s <= last_slot and order not in waited:
                waited.add(order)
                slots = pl.ds(first_slot, last_slot - first_slot + 1)
                wait_recv(gbuf.at[slots, pl.ds(0, RANKS - 1), *region(first_chunk, last_chunk)], r2.at[order])
        refresh(s)

    for i, chunk in enumerate(RETURN):
        rows, columns = cut(chunk)
        wait_recv(recv3[i].at[:, pl.ds(0, RANKS - 1)], r3.at[i])

        def pick(k, i=i):
            g = mp_peer(k)[1]
            return recv3[i][within(tab[SLOT_OF + g], OWN), within(tab[RANK_OF + g], RANKS)]

        recv4[i][0] = pick(0)

        def step4(k, carry, i=i, rows=rows, columns=columns, pick=pick):
            send4[k, rows, columns] = pick(k)
            remote(send4.at[k, rows, columns], recv4[i].at[k], s4, r4.at[i], mp_peer(k)).start()
            return carry

        lax.fori_loop(1, GROUPS, step4, 0)

    for i, chunk in enumerate(RETURN):
        rows, columns = cut(chunk)
        wait_recv(recv4[i].at[pl.ds(1, GROUPS - 1)], r4.at[i])

        def step5(j, carry, i=i, rows=rows, columns=columns):
            source = away(group, lax.rem(owner[group * GROUPS + j], GROUPS))
            outv[j, rows, columns] = recv4[i][within(source, GROUPS)]
            return carry

        lax.fori_loop(0, GROUPS, step5, 0)

    wait_send(send1.at[pl.ds(1, GROUPS - 1)], s1)
    wait_send(send2.at[pl.ds(1, RANKS - 1)], s2)
    wait_send(send3.at[:, pl.ds(0, RANKS - 1)], s3)
    wait_send(send4.at[pl.ds(1, GROUPS - 1)], s4)


def finish(*refs):
    count = len(refs) // 2
    copies = [pltpu.make_async_copy(refs[i], refs[count + i], refs[-1].at[i]) for i in range(count)]
    for copy in copies:
        copy.start()
    for copy in copies:
        copy.wait()


def body(gradient, owner, stat_left, stat_right, root_left, root_right):
    f32, bf16 = jnp.float32, jnp.bfloat16
    ng, nr = len(GATHER), len(RETURN)
    vmem, dma = pltpu.VMEM, pltpu.SemaphoreType.DMA
    anywhere = pl.BlockSpec(memory_space=pl.ANY)
    scratch = (
        [vmem((GROUPS, c[1], c[3]), f32) for c in GATHER]
        + [vmem((GROUPS, c[1], c[3]), f32) for c in GATHER]
        + [vmem((OWN, RANKS, c[1], c[3]), f32) for c in RETURN]
        + [vmem((GROUPS, c[1], c[3]), f32) for c in RETURN]
        + [
            vmem((GROUPS, ROWS, N), f32),
            vmem((RANKS, OWN, ROWS, N), f32),
            vmem((OWN, RANKS, ROWS, N), f32),
            vmem((OWN, RANKS, ROWS, N), f32),
            vmem((GROUPS, ROWS, N), f32),
            vmem((2, OWN, 2, N, N), bf16),
        ]
        + [dma((ng + 4,)), dma, dma((ng,)), dma, dma((len(INWARD),)), dma, dma((nr,)), dma, dma((nr,)), pltpu.SMEM((LIVE + SLOTS,), jnp.int32)]
    )
    args = (gradient, stat_left, stat_right, root_left, root_right)
    results = pl.pallas_call(
        kernel,
        out_shape=tuple(pltpu.VMEM(x.shape, x.dtype) for x in args),
        in_specs=[pl.BlockSpec(memory_space=pltpu.SMEM)] + [anywhere] * 5,
        out_specs=(pl.BlockSpec(memory_space=pltpu.VMEM),) * 5,
        scratch_shapes=scratch,
        compiler_params=pltpu.CompilerParams(
            collective_id=0, has_side_effects=True, vmem_limit_bytes=48 * 2**20
        ),
        cost_estimate=pl.CostEstimate(flops=75 * 2 * N**3, bytes_accessed=22 * 2**20, transcendentals=0),
        name="refresh",
    )(owner, *args)
    return pl.pallas_call(
        finish,
        out_shape=tuple(jax.ShapeDtypeStruct(x.shape, x.dtype) for x in args),
        in_specs=[pl.BlockSpec(memory_space=pltpu.VMEM)] * 5,
        out_specs=(anywhere,) * 5,
        scratch_shapes=[dma((5,))],
        compiler_params=pltpu.CompilerParams(vmem_limit_bytes=4 * 2**20),
        name="finish",
    )(*[pltpu.with_memory_space_constraint(x, pltpu.VMEM) for x in results])


def solution(mesh):
    state = P("dp", "mp", None, None, None)
    return jax.shard_map(
        body,
        mesh=mesh,
        in_specs=(P("mp", "dp", None), P(), state, state, state, state),
        out_specs=(P("mp", "dp", None), state, state, state, state),
        check_vma=False,
    )
```

```python
import functools

import jax
import jax.numpy as jnp
from jax import lax
from jax.experimental import pallas as pl
from jax.experimental.pallas import tpu as pltpu
from jax.sharding import PartitionSpec as P

MESH = pl.DeviceIdType.MESH
N = 512
ROWS = 64
OWN = 3
RANKS = 8
GROUPS = 16
SIDE = 4
GATHER = (
    (0, 8, 0, 256), (0, 8, 256, 256), (8, 8, 0, N), (16, 8, 0, N), (24, 8, 0, N), (32, 16, 0, N), (48, 16, 0, N),
)
RETURN = (
    (0, 8, 0, N), (8, 8, 0, N), (16, 16, 0, N), (32, 16, 0, N), (48, 8, 0, N), (56, 8, 0, 256), (56, 8, 256, 256),
)
INWARD = (
    (0, 0, 2, 0, 0), (1, 0, 2, 1, 1), (2, 0, 2, 2, 2), (3, 0, 2, 3, 3), (4, 0, 2, 4, 4),
    (5, 0, 1, 5, 5), (6, 0, 0, 6, 6), (6, 1, 1, 6, 6), (6, 2, 2, 5, 6),
)
PARTS = (((0, 64),), ((0, 64),), ((0, 16), (16, 48)))
OUTWARD = (
    (0, 0, 0, 0, 0), (0, 0, 0, 0, 1), (0, 0, 0, 0, 2), (1, 0, 1, 1, 0), (1, 0, 1, 1, 1), (1, 0, 1, 1, 2),
    (2, 0, 2, 2, 0), (2, 0, 2, 2, 1), (2, 1, 2, 2, 2), (2, 1, 0, 2, 3), (2, 1, 0, 2, 4), (2, 1, 0, 2, 5), (2, 1, 0, 2, 6),
)
AHEAD = 4
TINY = 2.0**-48

SLOTS = OWN * RANKS
SEND1, RANK_OF, SLOT_OF, SLOT2, LIVE = 0, GROUPS, 2 * GROUPS, 3 * GROUPS, 3 * GROUPS + SLOTS


def away(target, source):
    dz = lax.rem(lax.div(target, SIDE) - lax.div(source, SIDE) + SIDE, SIDE)
    dy = lax.rem(lax.rem(target, SIDE) - lax.rem(source, SIDE) + SIDE, SIDE)
    return dz * SIDE + dy


def within(index, size):
    return jnp.minimum(jnp.maximum(index, 0), size - 1)


def total(terms):
    return functools.reduce(lambda x, y: x + y, terms)


def cut(chunk):
    return pl.ds(chunk[0], chunk[1]), pl.ds(chunk[2], chunk[3])


def split(x):
    high = x.astype(jnp.bfloat16)
    return high, (x - high.astype(jnp.float32)).astype(jnp.bfloat16)


def dot(a, b):
    return jnp.dot(a, b, preferred_element_type=jnp.float32)


def dot3(a, b):
    (ah, al), (bh, bl) = a, b
    return dot(ah, bh) + (dot(ah, bl) + dot(al, bh))


def kernel(owner, grad, stat_l, stat_r, root_l, root_r, outv, new_sl, new_sr, new_rl, new_rr, *scratch):
    ng, nr = len(GATHER), len(RETURN)
    scratch = list(scratch)
    take = lambda count: [scratch.pop(0) for _ in range(count)]
    staged, recv1, recv3, recv4 = take(ng), take(ng), take(nr), take(nr)
    send1, send2, gbuf, send3, send4, x5 = take(6)
    in_sem, s1, r1, s2, r2, s3, r3, s4, r4, tab = take(10)

    st, rt = (new_sl.at[0, 0], new_sr.at[0, 0]), (new_rl.at[0, 0], new_rr.at[0, 0])
    rank, group = lax.axis_index("dp"), lax.axis_index("mp")
    z, y = group // SIDE, group % SIDE

    def mp_peer(k):
        return (rank, ((z + k // SIDE) % SIDE) * SIDE + (y + k % SIDE) % SIDE)

    def dp_peer(d):
        return ((rank + d) % RANKS, group)

    def remote(src, dst, ssem, rsem, peer):
        return pltpu.make_async_remote_copy(
            src_ref=src, dst_ref=dst, send_sem=ssem, recv_sem=rsem, device_id=peer, device_id_type=MESH
        )

    def wait_recv(region, sem):
        remote(region, region, s1, sem, dp_peer(1)).wait_recv()

    def wait_send(region, sem):
        remote(region, region, sem, r1.at[0], dp_peer(1)).wait_send()

    grad_in = [
        pltpu.make_async_copy(grad.at[:, *cut(chunk)], staged[i], in_sem.at[i]) for i, chunk in enumerate(GATHER)
    ]
    state_in = [
        pltpu.make_async_copy(src.at[0, 0], dst, in_sem.at[ng + i])
        for i, (src, dst) in enumerate(
            ((root_l, rt[0]), (root_r, rt[1]), (stat_l, st[0]), (stat_r, st[1]))
        )
    ]
    for copy in grad_in + state_in:
        copy.start()

    def choose_first(k, carry):
        target = mp_peer(k)[1]
        tab[SEND1 + k] = total(
            jnp.where(lax.rem(owner[group * GROUPS + j], GROUPS) == target, j, 0) for j in range(GROUPS)
        )
        return carry

    def choose_rank(g, carry):
        here = [owner[g * GROUPS + j] for j in range(GROUPS)]
        tab[RANK_OF + g] = total(jnp.where(lax.rem(o, GROUPS) == group, lax.div(o, GROUPS), 0) for o in here)
        return carry

    def choose_slot(g, carry):
        mine = tab[RANK_OF + g]
        tab[SLOT_OF + g] = total(
            jnp.where((tab[RANK_OF + c] == mine) & (c < g), 1, 0) for c in range(GROUPS)
        )
        return carry

    def choose_second(p, carry):
        places = [tab[RANK_OF + g] * OWN + tab[SLOT_OF + g] for g in range(GROUPS)]
        tab[SLOT2 + p] = total(jnp.where(places[g] == p, away(group, g), 0) for g in range(GROUPS))
        tab[LIVE + p] = total(jnp.where(places[g] == p, 1, 0) for g in range(GROUPS))
        return carry

    barrier = pltpu.get_barrier_semaphore()

    def greet_mp(k, carry):
        pl.semaphore_signal(barrier, inc=1, device_id=mp_peer(k), device_id_type=MESH)
        return carry

    def greet_dp(d, carry):
        pl.semaphore_signal(barrier, inc=1, device_id=dp_peer(d), device_id_type=MESH)
        return carry

    lax.fori_loop(1, GROUPS, greet_mp, 0)
    lax.fori_loop(1, RANKS, greet_dp, 0)
    lax.fori_loop(0, GROUPS, choose_first, 0)
    pl.semaphore_wait(barrier, GROUPS - 1 + RANKS - 1)

    def first(i):
        grad_in[i].wait()
        rows, columns = cut(GATHER[i])
        recv1[i][0] = staged[i][within(tab[SEND1], GROUPS)]

        def step1(k, carry):
            send1[k, rows, columns] = staged[i][within(tab[SEND1 + k], GROUPS)]
            remote(send1.at[k, rows, columns], recv1[i].at[k], s1, r1.at[i], mp_peer(k)).start()
            return carry

        lax.fori_loop(1, GROUPS, step1, 0)

    def region(first_chunk, last_chunk):
        start = GATHER[first_chunk][0]
        end = GATHER[last_chunk][0] + GATHER[last_chunk][1]
        columns = GATHER[first_chunk][2:] if first_chunk == last_chunk else (0, N)
        return cut((start, end - start, *columns))

    def second(i):
        rows, columns = cut(GATHER[i])

        def fill(d, carry):
            peer = (rank + d) % RANKS
            for s in range(OWN):
                send2[d, s, rows, columns] = recv1[i][within(tab[SLOT2 + peer * OWN + s], GROUPS)]
            return carry

        for order, (after, first_slot, last_slot, first_chunk, last_chunk) in enumerate(INWARD):
            if after != i:
                continue
            slots, part = pl.ds(first_slot, last_slot - first_slot + 1), region(first_chunk, last_chunk)

            def step2(d, carry, order=order, slots=slots, part=part, filled=fill):
                if filled is not None:
                    filled(d, carry)
                remote(
                    send2.at[d, slots, *part], gbuf.at[slots, rank, *part], s2, r2.at[order], dp_peer(d)
                ).start()
                return carry

            lax.fori_loop(1, RANKS, step2, 0)
            fill = None

    def own_rows(i):
        rows, columns = cut(GATHER[i])
        for s in range(OWN):
            gbuf[s, rank, rows, columns] = recv1[i][within(tab[SLOT2 + rank * OWN + s], GROUPS)]

    def power(t):
        side = t % 2
        s = t // 2
        x = rt[side][s]
        sq = split(dot(x, x))
        fourth = split(dot3(sq, sq) * TINY)
        high, low = split(dot(x, fourth[0]) + dot(x, fourth[1]))
        x5[side, s, 0] = high
        x5[side, s, 1] = low

    for i in range(AHEAD):
        first(i)
    lax.fori_loop(0, GROUPS, choose_rank, 0)
    lax.fori_loop(0, GROUPS, choose_slot, 0)
    lax.fori_loop(0, SLOTS, choose_second, 0)
    for i in range(ng):
        wait_recv(recv1[i].at[pl.ds(1, GROUPS - 1)], r1.at[i])
        second(i)
        if i + AHEAD < ng:
            first(i + AHEAD)
        own_rows(i)
        if i == 0:
            state_in[0].wait()
            state_in[1].wait()
        if i >= ng - 2 * OWN:
            power(i - (ng - 2 * OWN))
    state_in[2].wait()
    state_in[3].wait()

    eye = lax.broadcasted_iota(jnp.int32, (N, N), 0) == lax.broadcasted_iota(jnp.int32, (N, N), 1)

    def shift(side, s, new, taken):
        scale = jnp.sum(jnp.where(eye, new, 0.0)) / N
        st[side][s] = jnp.where(taken, new, 0.0)
        return split(new / scale + jnp.where(eye, 0.001, 0.0))

    def rows_of(x, part):
        return x.reshape(RANKS, ROWS, N)[:, part[0] : sum(part)].reshape(RANKS * part[1], N)

    def newton(side, s, shifted, taken, part):
        high, low = (rows_of(x5[side, s, i], part) for i in range(2))
        moved = dot3((high, low), shifted)
        inverse = 1.25 * rows_of(rt[side][s], part).astype(jnp.float32) - (0.25 / TINY) * moved
        kept = jnp.where(taken, inverse, 0.0).astype(jnp.bfloat16)
        if part == (0, ROWS):
            rt[side][s] = kept
        else:
            for e in range(RANKS):
                rt[side][s, pl.ds(e * ROWS + part[0], part[1]), :] = kept[e * part[1] : (e + 1) * part[1]]
        return split(inverse)

    def refresh(s):
        taken = tab[LIVE + rank * OWN + s] > 0
        g32 = gbuf[s].reshape(N, N)
        g, gt = split(g32), split(g32.T)
        shifted_r = shift(1, s, 0.95 * st[1][s] + dot3(gt, g), taken)
        inv_r = newton(1, s, shifted_r, taken, (0, ROWS))
        shifted_l = shift(0, s, 0.95 * st[0][s] + dot3(g, gt), taken)
        for p, part in enumerate(PARTS[s]):
            inv_l = newton(0, s, shifted_l, taken, part)
            result = dot3(split(dot3(inv_l, g)), inv_r)
            send3[s, :, pl.ds(*part), :] = result.reshape(RANKS, part[1], N)
            for after, after_part, first_slot, last_slot, chunk in OUTWARD:
                if (after, after_part) == (s, p):
                    back(chunk, first_slot, last_slot - first_slot + 1)

    def back(i, first, count):
        (rows, columns), some = cut(RETURN[i]), pl.ds(first, count)

        def step3(d, carry):
            peer = (rank + d) % RANKS
            remote(send3.at[some, peer, rows, columns], recv3[i].at[some, rank], s3, r3.at[i], dp_peer(d)).start()
            return carry

        lax.fori_loop(1, RANKS, step3, 0)
        for s in range(first, first + count):
            recv3[i][s, rank] = send3[s, rank, rows, columns]

    waited = set()
    for s in range(OWN):
        for order, (_, first_slot, last_slot, first_chunk, last_chunk) in enumerate(INWARD):
            if first_slot <= s <= last_slot and order not in waited:
                waited.add(order)
                slots = pl.ds(first_slot, last_slot - first_slot + 1)
                wait_recv(gbuf.at[slots, pl.ds(0, RANKS - 1), *region(first_chunk, last_chunk)], r2.at[order])
        refresh(s)

    for i, chunk in enumerate(RETURN):
        rows, columns = cut(chunk)
        wait_recv(recv3[i].at[:, pl.ds(0, RANKS - 1)], r3.at[i])

        def pick(k, i=i):
            g = mp_peer(k)[1]
            return recv3[i][within(tab[SLOT_OF + g], OWN), within(tab[RANK_OF + g], RANKS)]

        recv4[i][0] = pick(0)

        def step4(k, carry, i=i, rows=rows, columns=columns, pick=pick):
            send4[k, rows, columns] = pick(k)
            remote(send4.at[k, rows, columns], recv4[i].at[k], s4, r4.at[i], mp_peer(k)).start()
            return carry

        lax.fori_loop(1, GROUPS, step4, 0)

    for i, chunk in enumerate(RETURN):
        rows, columns = cut(chunk)
        wait_recv(recv4[i].at[pl.ds(1, GROUPS - 1)], r4.at[i])

        def step5(j, carry, i=i, rows=rows, columns=columns):
            source = away(group, lax.rem(owner[group * GROUPS + j], GROUPS))
            outv[j, rows, columns] = recv4[i][within(source, GROUPS)]
            return carry

        lax.fori_loop(0, GROUPS, step5, 0)

    wait_send(send1.at[pl.ds(1, GROUPS - 1)], s1)
    wait_send(send2.at[pl.ds(1, RANKS - 1)], s2)
    wait_send(send3.at[:, pl.ds(0, RANKS - 1)], s3)
    wait_send(send4.at[pl.ds(1, GROUPS - 1)], s4)


def finish(*refs):
    count = len(refs) // 2
    copies = [pltpu.make_async_copy(refs[i], refs[count + i], refs[-1].at[i]) for i in range(count)]
    for copy in copies:
        copy.start()
    for copy in copies:
        copy.wait()


def body(gradient, owner, stat_left, stat_right, root_left, root_right):
    f32, bf16 = jnp.float32, jnp.bfloat16
    ng, nr = len(GATHER), len(RETURN)
    vmem, dma = pltpu.VMEM, pltpu.SemaphoreType.DMA
    anywhere = pl.BlockSpec(memory_space=pl.ANY)
    scratch = (
        [vmem((GROUPS, c[1], c[3]), f32) for c in GATHER]
        + [vmem((GROUPS, c[1], c[3]), f32) for c in GATHER]
        + [vmem((OWN, RANKS, c[1], c[3]), f32) for c in RETURN]
        + [vmem((GROUPS, c[1], c[3]), f32) for c in RETURN]
        + [
            vmem((GROUPS, ROWS, N), f32),
            vmem((RANKS, OWN, ROWS, N), f32),
            vmem((OWN, RANKS, ROWS, N), f32),
            vmem((OWN, RANKS, ROWS, N), f32),
            vmem((GROUPS, ROWS, N), f32),
            vmem((2, OWN, 2, N, N), bf16),
        ]
        + [dma((ng + 4,)), dma, dma((ng,)), dma, dma((len(INWARD),)), dma, dma((nr,)), dma, dma((nr,)), pltpu.SMEM((LIVE + SLOTS,), jnp.int32)]
    )
    args = (gradient, stat_left, stat_right, root_left, root_right)
    results = pl.pallas_call(
        kernel,
        out_shape=tuple(pltpu.VMEM(x.shape, x.dtype) for x in args),
        in_specs=[pl.BlockSpec(memory_space=pltpu.SMEM)] + [anywhere] * 5,
        out_specs=(pl.BlockSpec(memory_space=pltpu.VMEM),) * 5,
        scratch_shapes=scratch,
        compiler_params=pltpu.CompilerParams(
            collective_id=0, has_side_effects=True, vmem_limit_bytes=48 * 2**20
        ),
        cost_estimate=pl.CostEstimate(flops=75 * 2 * N**3, bytes_accessed=22 * 2**20, transcendentals=0),
        name="refresh",
    )(owner, *args)
    return pl.pallas_call(
        finish,
        out_shape=tuple(jax.ShapeDtypeStruct(x.shape, x.dtype) for x in args),
        in_specs=[pl.BlockSpec(memory_space=pltpu.VMEM)] * 5,
        out_specs=(anywhere,) * 5,
        scratch_shapes=[dma((5,))],
        compiler_params=pltpu.CompilerParams(vmem_limit_bytes=4 * 2**20),
        name="finish",
    )(*[pltpu.with_memory_space_constraint(x, pltpu.VMEM) for x in results])


def solution(mesh):
    state = P("dp", "mp", None, None, None)
    return jax.shard_map(
        body,
        mesh=mesh,
        in_specs=(P("mp", "dp", None), P(), state, state, state, state),
        out_specs=(P("mp", "dp", None), state, state, state, state),
        check_vma=False,
    )
```

```python
import functools

import jax
import jax.numpy as jnp
from jax import lax
from jax.experimental import pallas as pl
from jax.experimental.pallas import tpu as pltpu
from jax.sharding import PartitionSpec as P

MESH = pl.DeviceIdType.MESH
N = 512
ROWS = 64
OWN = 3
RANKS = 8
GROUPS = 16
SIDE = 4
GATHER = (
    (0, 8, 0, 256), (0, 8, 256, 256), (8, 8, 0, N), (16, 8, 0, N), (24, 8, 0, N), (32, 16, 0, N), (48, 16, 0, N),
)
RETURN = (
    (0, 8, 0, N), (8, 8, 0, N), (16, 16, 0, N), (32, 16, 0, N), (48, 8, 0, N), (56, 8, 0, 256), (56, 8, 256, 256),
)
INWARD = (
    (0, 0, 2, 0, 0), (1, 0, 2, 1, 1), (2, 0, 2, 2, 2), (3, 0, 2, 3, 3), (4, 0, 2, 4, 4),
    (5, 0, 1, 5, 5), (6, 0, 0, 6, 6), (6, 1, 1, 6, 6), (6, 2, 2, 5, 6),
)
PARTS = (((0, 64),), ((0, 64),), ((0, 16), (16, 48)))
OUTWARD = (
    (0, 0, 0, 0, 0), (0, 0, 0, 0, 1), (0, 0, 0, 0, 2), (1, 0, 1, 1, 0), (1, 0, 1, 1, 1), (1, 0, 1, 1, 2),
    (2, 0, 2, 2, 0), (2, 0, 2, 2, 1), (2, 1, 2, 2, 2), (2, 1, 0, 2, 3), (2, 1, 0, 2, 4), (2, 1, 0, 2, 5), (2, 1, 0, 2, 6),
)
AHEAD = 4
TINY = 2.0**-48

SLOTS = OWN * RANKS
SEND1, RANK_OF, SLOT_OF, SLOT2, LIVE = 0, GROUPS, 2 * GROUPS, 3 * GROUPS, 3 * GROUPS + SLOTS


def away(target, source):
    dz = lax.rem(lax.div(target, SIDE) - lax.div(source, SIDE) + SIDE, SIDE)
    dy = lax.rem(lax.rem(target, SIDE) - lax.rem(source, SIDE) + SIDE, SIDE)
    return dz * SIDE + dy


def within(index, size):
    return jnp.minimum(jnp.maximum(index, 0), size - 1)


def total(terms):
    return functools.reduce(lambda x, y: x + y, terms)


def cut(chunk):
    return pl.ds(chunk[0], chunk[1]), pl.ds(chunk[2], chunk[3])


def split(x):
    high = x.astype(jnp.bfloat16)
    return high, (x - high.astype(jnp.float32)).astype(jnp.bfloat16)


def dot(a, b):
    return jnp.dot(a, b, preferred_element_type=jnp.float32)


def dot3(a, b):
    (ah, al), (bh, bl) = a, b
    return dot(ah, bh) + (dot(ah, bl) + dot(al, bh))


def kernel(owner, grad, stat_l, stat_r, root_l, root_r, outv, new_sl, new_sr, new_rl, new_rr, *scratch):
    ng, nr = len(GATHER), len(RETURN)
    scratch = list(scratch)
    take = lambda count: [scratch.pop(0) for _ in range(count)]
    staged, recv1, recv3, recv4 = take(ng), take(ng), take(nr), take(nr)
    send1, send2, gbuf, send3, send4, x5 = take(6)
    in_sem, s1, r1, s2, r2, s3, r3, s4, r4, tab = take(10)

    st, rt = (new_sl.at[0, 0], new_sr.at[0, 0]), (new_rl.at[0, 0], new_rr.at[0, 0])
    rank, group = lax.axis_index("dp"), lax.axis_index("mp")
    z, y = group // SIDE, group % SIDE

    def mp_peer(k):
        return (rank, ((z + k // SIDE) % SIDE) * SIDE + (y + k % SIDE) % SIDE)

    def dp_peer(d):
        return ((rank + d) % RANKS, group)

    def remote(src, dst, ssem, rsem, peer):
        return pltpu.make_async_remote_copy(
            src_ref=src, dst_ref=dst, send_sem=ssem, recv_sem=rsem, device_id=peer, device_id_type=MESH
        )

    def wait_recv(region, sem):
        remote(region, region, s1, sem, dp_peer(1)).wait_recv()

    def wait_send(region, sem):
        remote(region, region, sem, r1.at[0], dp_peer(1)).wait_send()

    grad_in = [
        pltpu.make_async_copy(grad.at[:, *cut(chunk)], staged[i], in_sem.at[i]) for i, chunk in enumerate(GATHER)
    ]
    state_in = [
        pltpu.make_async_copy(src.at[0, 0], dst, in_sem.at[ng + i])
        for i, (src, dst) in enumerate(
            ((root_l, rt[0]), (root_r, rt[1]), (stat_l, st[0]), (stat_r, st[1]))
        )
    ]
    for copy in grad_in + state_in:
        copy.start()

    def choose_first(k, carry):
        target = mp_peer(k)[1]
        tab[SEND1 + k] = total(
            jnp.where(lax.rem(owner[group * GROUPS + j], GROUPS) == target, j, 0) for j in range(GROUPS)
        )
        return carry

    def choose_rank(g, carry):
        here = [owner[g * GROUPS + j] for j in range(GROUPS)]
        tab[RANK_OF + g] = total(jnp.where(lax.rem(o, GROUPS) == group, lax.div(o, GROUPS), 0) for o in here)
        return carry

    def choose_slot(g, carry):
        mine = tab[RANK_OF + g]
        tab[SLOT_OF + g] = total(
            jnp.where((tab[RANK_OF + c] == mine) & (c < g), 1, 0) for c in range(GROUPS)
        )
        return carry

    def choose_second(p, carry):
        places = [tab[RANK_OF + g] * OWN + tab[SLOT_OF + g] for g in range(GROUPS)]
        tab[SLOT2 + p] = total(jnp.where(places[g] == p, away(group, g), 0) for g in range(GROUPS))
        tab[LIVE + p] = total(jnp.where(places[g] == p, 1, 0) for g in range(GROUPS))
        return carry

    barrier = pltpu.get_barrier_semaphore()

    def greet_mp(k, carry):
        pl.semaphore_signal(barrier, inc=1, device_id=mp_peer(k), device_id_type=MESH)
        return carry

    def greet_dp(d, carry):
        pl.semaphore_signal(barrier, inc=1, device_id=dp_peer(d), device_id_type=MESH)
        return carry

    lax.fori_loop(1, GROUPS, greet_mp, 0)
    lax.fori_loop(1, RANKS, greet_dp, 0)
    lax.fori_loop(0, GROUPS, choose_first, 0)
    pl.semaphore_wait(barrier, GROUPS - 1 + RANKS - 1)

    def first(i):
        grad_in[i].wait()
        rows, columns = cut(GATHER[i])

        def step1(k, carry):
            send1[k, rows, columns] = staged[i][within(tab[SEND1 + k], GROUPS)]
            remote(send1.at[k, rows, columns], recv1[i].at[k], s1, r1.at[i], mp_peer(k)).start()
            return carry

        lax.fori_loop(1, GROUPS, step1, 0, unroll=True)
        recv1[i][0] = staged[i][within(tab[SEND1], GROUPS)]

    def region(first_chunk, last_chunk):
        start = GATHER[first_chunk][0]
        end = GATHER[last_chunk][0] + GATHER[last_chunk][1]
        columns = GATHER[first_chunk][2:] if first_chunk == last_chunk else (0, N)
        return cut((start, end - start, *columns))

    def second(i):
        rows, columns = cut(GATHER[i])

        def fill(d, carry):
            peer = (rank + d) % RANKS
            for s in range(OWN):
                send2[d, s, rows, columns] = recv1[i][within(tab[SLOT2 + peer * OWN + s], GROUPS)]
            return carry

        for order, (after, first_slot, last_slot, first_chunk, last_chunk) in enumerate(INWARD):
            if after != i:
                continue
            slots, part = pl.ds(first_slot, last_slot - first_slot + 1), region(first_chunk, last_chunk)

            def step2(d, carry, order=order, slots=slots, part=part, filled=fill):
                if filled is not None:
                    filled(d, carry)
                remote(
                    send2.at[d, slots, *part], gbuf.at[slots, rank, *part], s2, r2.at[order], dp_peer(d)
                ).start()
                return carry

            lax.fori_loop(1, RANKS, step2, 0)
            fill = None

    def own_rows(i):
        rows, columns = cut(GATHER[i])
        for s in range(OWN):
            gbuf[s, rank, rows, columns] = recv1[i][within(tab[SLOT2 + rank * OWN + s], GROUPS)]

    def power(t):
        side = t % 2
        s = t // 2
        x = rt[side][s]
        sq = split(dot(x, x))
        fourth = split(dot3(sq, sq) * TINY)
        high, low = split(dot(x, fourth[0]) + dot(x, fourth[1]))
        x5[side, s, 0] = high
        x5[side, s, 1] = low

    for i in range(AHEAD):
        first(i)
    lax.fori_loop(0, GROUPS, choose_rank, 0)
    lax.fori_loop(0, GROUPS, choose_slot, 0)
    lax.fori_loop(0, SLOTS, choose_second, 0)
    for i in range(ng):
        wait_recv(recv1[i].at[pl.ds(1, GROUPS - 1)], r1.at[i])
        second(i)
        if i + AHEAD < ng:
            first(i + AHEAD)
        own_rows(i)
        if i == 0:
            state_in[0].wait()
            state_in[1].wait()
        if i >= ng - 2 * OWN:
            power(i - (ng - 2 * OWN))
    state_in[2].wait()
    state_in[3].wait()

    eye = lax.broadcasted_iota(jnp.int32, (N, N), 0) == lax.broadcasted_iota(jnp.int32, (N, N), 1)

    def shift(side, s, new, taken):
        scale = jnp.sum(jnp.where(eye, new, 0.0)) / N
        st[side][s] = jnp.where(taken, new, 0.0)
        return split(new / scale + jnp.where(eye, 0.001, 0.0))

    def rows_of(x, part):
        return x.reshape(RANKS, ROWS, N)[:, part[0] : sum(part)].reshape(RANKS * part[1], N)

    def newton(side, s, shifted, taken, part):
        high, low = (rows_of(x5[side, s, i], part) for i in range(2))
        moved = dot3((high, low), shifted)
        inverse = 1.25 * rows_of(rt[side][s], part).astype(jnp.float32) - (0.25 / TINY) * moved
        kept = jnp.where(taken, inverse, 0.0).astype(jnp.bfloat16)
        if part == (0, ROWS):
            rt[side][s] = kept
        else:
            for e in range(RANKS):
                rt[side][s, pl.ds(e * ROWS + part[0], part[1]), :] = kept[e * part[1] : (e + 1) * part[1]]
        return split(inverse)

    def refresh(s):
        taken = tab[LIVE + rank * OWN + s] > 0
        g32 = gbuf[s].reshape(N, N)
        g, gt = split(g32), split(g32.T)
        shifted_r = shift(1, s, 0.95 * st[1][s] + dot3(gt, g), taken)
        inv_r = newton(1, s, shifted_r, taken, (0, ROWS))
        shifted_l = shift(0, s, 0.95 * st[0][s] + dot3(g, gt), taken)
        for p, part in enumerate(PARTS[s]):
            inv_l = newton(0, s, shifted_l, taken, part)
            result = dot3(split(dot3(inv_l, g)), inv_r)
            send3[s, :, pl.ds(*part), :] = result.reshape(RANKS, part[1], N)
            for after, after_part, first_slot, last_slot, chunk in OUTWARD:
                if (after, after_part) == (s, p):
                    back(chunk, first_slot, last_slot - first_slot + 1)

    def back(i, first, count):
        (rows, columns), some = cut(RETURN[i]), pl.ds(first, count)

        def step3(d, carry):
            peer = (rank + d) % RANKS
            remote(send3.at[some, peer, rows, columns], recv3[i].at[some, rank], s3, r3.at[i], dp_peer(d)).start()
            return carry

        lax.fori_loop(1, RANKS, step3, 0)
        for s in range(first, first + count):
            recv3[i][s, rank] = send3[s, rank, rows, columns]

    waited = set()
    for s in range(OWN):
        for order, (_, first_slot, last_slot, first_chunk, last_chunk) in enumerate(INWARD):
            if first_slot <= s <= last_slot and order not in waited:
                waited.add(order)
                slots = pl.ds(first_slot, last_slot - first_slot + 1)
                wait_recv(gbuf.at[slots, pl.ds(0, RANKS - 1), *region(first_chunk, last_chunk)], r2.at[order])
        refresh(s)

    for i, chunk in enumerate(RETURN):
        rows, columns = cut(chunk)
        wait_recv(recv3[i].at[:, pl.ds(0, RANKS - 1)], r3.at[i])

        def pick(k, i=i):
            g = mp_peer(k)[1]
            return recv3[i][within(tab[SLOT_OF + g], OWN), within(tab[RANK_OF + g], RANKS)]


        def step4(k, carry, i=i, rows=rows, columns=columns, pick=pick):
            send4[k, rows, columns] = pick(k)
            remote(send4.at[k, rows, columns], recv4[i].at[k], s4, r4.at[i], mp_peer(k)).start()
            return carry

        lax.fori_loop(1, GROUPS, step4, 0, unroll=True)
        recv4[i][0] = pick(0)

    for i, chunk in enumerate(RETURN):
        rows, columns = cut(chunk)
        wait_recv(recv4[i].at[pl.ds(1, GROUPS - 1)], r4.at[i])

        def step5(j, carry, i=i, rows=rows, columns=columns):
            source = away(group, lax.rem(owner[group * GROUPS + j], GROUPS))
            outv[j, rows, columns] = recv4[i][within(source, GROUPS)]
            return carry

        lax.fori_loop(0, GROUPS, step5, 0)

    wait_send(send1.at[pl.ds(1, GROUPS - 1)], s1)
    wait_send(send2.at[pl.ds(1, RANKS - 1)], s2)
    wait_send(send3.at[:, pl.ds(0, RANKS - 1)], s3)
    wait_send(send4.at[pl.ds(1, GROUPS - 1)], s4)


def finish(*refs):
    count = len(refs) // 2
    copies = [pltpu.make_async_copy(refs[i], refs[count + i], refs[-1].at[i]) for i in range(count)]
    for copy in copies:
        copy.start()
    for copy in copies:
        copy.wait()


def body(gradient, owner, stat_left, stat_right, root_left, root_right):
    f32, bf16 = jnp.float32, jnp.bfloat16
    ng, nr = len(GATHER), len(RETURN)
    vmem, dma = pltpu.VMEM, pltpu.SemaphoreType.DMA
    anywhere = pl.BlockSpec(memory_space=pl.ANY)
    scratch = (
        [vmem((GROUPS, c[1], c[3]), f32) for c in GATHER]
        + [vmem((GROUPS, c[1], c[3]), f32) for c in GATHER]
        + [vmem((OWN, RANKS, c[1], c[3]), f32) for c in RETURN]
        + [vmem((GROUPS, c[1], c[3]), f32) for c in RETURN]
        + [
            vmem((GROUPS, ROWS, N), f32),
            vmem((RANKS, OWN, ROWS, N), f32),
            vmem((OWN, RANKS, ROWS, N), f32),
            vmem((OWN, RANKS, ROWS, N), f32),
            vmem((GROUPS, ROWS, N), f32),
            vmem((2, OWN, 2, N, N), bf16),
        ]
        + [dma((ng + 4,)), dma, dma((ng,)), dma, dma((len(INWARD),)), dma, dma((nr,)), dma, dma((nr,)), pltpu.SMEM((LIVE + SLOTS,), jnp.int32)]
    )
    args = (gradient, stat_left, stat_right, root_left, root_right)
    results = pl.pallas_call(
        kernel,
        out_shape=tuple(pltpu.VMEM(x.shape, x.dtype) for x in args),
        in_specs=[pl.BlockSpec(memory_space=pltpu.SMEM)] + [anywhere] * 5,
        out_specs=(pl.BlockSpec(memory_space=pltpu.VMEM),) * 5,
        scratch_shapes=scratch,
        compiler_params=pltpu.CompilerParams(
            collective_id=0, has_side_effects=True, vmem_limit_bytes=48 * 2**20
        ),
        cost_estimate=pl.CostEstimate(flops=75 * 2 * N**3, bytes_accessed=22 * 2**20, transcendentals=0),
        name="refresh",
    )(owner, *args)
    return pl.pallas_call(
        finish,
        out_shape=tuple(jax.ShapeDtypeStruct(x.shape, x.dtype) for x in args),
        in_specs=[pl.BlockSpec(memory_space=pltpu.VMEM)] * 5,
        out_specs=(anywhere,) * 5,
        scratch_shapes=[dma((5,))],
        compiler_params=pltpu.CompilerParams(vmem_limit_bytes=4 * 2**20),
        name="finish",
    )(*[pltpu.with_memory_space_constraint(x, pltpu.VMEM) for x in results])


def solution(mesh):
    state = P("dp", "mp", None, None, None)
    return jax.shard_map(
        body,
        mesh=mesh,
        in_specs=(P("mp", "dp", None), P(), state, state, state, state),
        out_specs=(P("mp", "dp", None), state, state, state, state),
        check_vma=False,
    )
```
